128 devices in a mesh: gx: 8 (over y_lo, z), gy: 16 (over y_hi, x, core).
Axes of the slice: x: 4, y: 4 (y_hi: 2, y_lo: 2; y = y_hi * 2 + y_lo), z: 4, core: 2. Of those that a mesh axis runs over, the one named last changes fastest.
Arguments:
- state: float32 [4, 256, 512, 128], P(None, 'gx', 'gy'), may hold values from 0 to 1
- velocity: float32 [3, 256, 512, 128], P(None, 'gx', 'gy'), may hold values from -1 to 1
- routes: int32 [16, 32, 8], P('gx', 'gy'), may hold values from -1 to 223, as said below
- w_in: bfloat16 [128, 7], replicated, may hold values from -2 to 2
- w_mid: bfloat16 [128, 128], replicated, may hold values from -0.5 to 0.5
- w_deep: bfloat16 [128, 128], replicated, may hold values from -0.5 to 0.5
- w_out: bfloat16 [4, 128], replicated, may hold values from -1.5 to 1.5
Outputs:
- evolved: float32 [4, 256, 512, 128], P(None, 'gx', 'gy')
The draws below stay inside these ranges and needn't reach their ends.
Inputs may be any that keep to these rules, and one draw needn't show every extreme that they name: `routes`: -1 for a block outside the interface band; for a band block d * 14 + s, where d is the gy index of the device with the same gx index that evaluates its closure and s its place there. Each device receives exactly 14 band blocks from the devices of its gy group, in distinct places, and at most 2 from any one device.
All inputs are finite; a program needn't handle non-finite values.
Results may differ from the reference program's by a relative error of at most 0.0008.
Values may be sent and summed in bfloat16 or wider, within the bound.
No kernel may reach another device: no remote copies, remote signals or barrier semaphores. Data moves between devices by JAX's collectives and lax.ppermute only.
A program may use at most 128 MiB of HBM per device.

```python
import jax
import jax.numpy as jnp
from jax import lax

NV = 4
NF = 7
HID = 128
BS = 16
BX = 2
BY = 2
NBZ = 8
SLOTS = 14
NX = 256
NY = 512
NZ = 128
NBAND = 1792
N_GX = 8
N_GY = 16


def draw_routes(key, part):
    key = jax.random.fold_in(key, 11)
    group_size = N_GY
    block_count = BX * BY * NBZ
    remaining = group_size * SLOTS - block_count

    def draw_group(group_key):
        busy_key, order_key = jax.random.split(group_key)
        busiest = jax.random.randint(busy_key, (), 0, group_size)
        ranking = jax.random.permutation(order_key, (group_size - 1) * block_count)
        others = (ranking < remaining).astype(jnp.int32).reshape(group_size - 1, block_count)
        empty_row = jnp.zeros((1, block_count), jnp.int32)
        lower_rows = jnp.concatenate([others, empty_row], axis=0)
        upper_rows = jnp.concatenate([empty_row, others], axis=0)
        row_index = jnp.arange(group_size)[:, None]
        in_band = jnp.where(row_index < busiest, lower_rows, jnp.where(row_index == busiest, 1, upper_rows))
        band_flat = in_band.reshape(-1)
        position = jnp.cumsum(band_flat) - band_flat
        route_code = position % group_size * SLOTS + position // group_size
        return jnp.where(band_flat > 0, route_code, -1).reshape(group_size, block_count)
    routes = jax.vmap(draw_group)(jax.random.split(key, N_GX))
    routes = routes.reshape(N_GX, N_GY, BX, BY, NBZ).transpose(0, 2, 1, 3, 4)
    return routes.reshape(N_GX * BX, N_GY * BY, NBZ).astype(jnp.int32)


def levels(rng, shape, cuts, least, top_value):
    def one(dim, parts):
        draws = jax.random.uniform(jax.random.fold_in(jax.random.fold_in(rng, 6), dim), (parts,), jnp.float32, least / len(cuts), top_value / len(cuts))
        return jnp.repeat(jnp.exp(draws), shape[dim] // parts).reshape((-1,) + (1,) * (len(shape) - dim - 1))

    loudness = one(*cuts[0])
    for cut in cuts[1:]:
        loudness = loudness * one(*cut)
    return loudness


def bell_draw(own_key, dims, width, reach, dtype=jnp.bfloat16):
    result = width * jax.random.normal(own_key, dims, jnp.float32)
    return jnp.clip(result, min=-reach, max=reach).astype(dtype)


def setup_inputs(seed: int = 0) -> dict:
    seeds = jax.random.split(jax.random.key(seed), 8)
    return {
        "state": jnp.clip(1.0 * jax.random.uniform(seeds[0], (NV, NX, NY, NZ), jnp.float32) ** levels(seeds[0], (NV, NX, NY, NZ), ((1, 8), (2, 16)), -0.2, 0.2), 0.0, 1.0),
        "velocity": jnp.clip(jax.random.uniform(seeds[1], (3, NX, NY, NZ), jnp.float32, -1.0, 1.0) * levels(seeds[1], (3, NX, NY, NZ), ((1, 8), (2, 16)), -0.4, 0.0), -1.0, 1.0),
        "routes": draw_routes(jax.random.fold_in(seeds[7], 71), 0),
        "w_in": bell_draw(seeds[3], (HID, NF), NF ** -0.5, 2.0),
        "w_mid": bell_draw(seeds[4], (HID, HID), HID ** -0.5, 0.5),
        "w_deep": bell_draw(seeds[5], (HID, HID), HID ** -0.5, 0.5),
        "w_out": bell_draw(seeds[6], (NV, HID), (HID // 8) ** -0.5, 1.5),
    }


EPS = 1e-6
STEP = 0.25


def weno_face(far_left, near_left, centre, near_right, far_right):
    smooth_zero = 13.0 / 12.0 * (far_left - 2.0 * near_left + centre) ** 2 + 0.25 * (far_left - 4.0 * near_left + 3.0 * centre) ** 2
    smooth_one = 13.0 / 12.0 * (near_left - 2.0 * centre + near_right) ** 2 + 0.25 * (near_left - near_right) ** 2
    smooth_two = 13.0 / 12.0 * (centre - 2.0 * near_right + far_right) ** 2 + 0.25 * (3.0 * centre - 4.0 * near_right + far_right) ** 2
    weight_zero = 0.1 / (EPS + smooth_zero) ** 2
    weight_one = 0.6 / (EPS + smooth_one) ** 2
    weight_two = 0.3 / (EPS + smooth_two) ** 2
    guess_zero = (2.0 * far_left - 7.0 * near_left + 11.0 * centre) / 6.0
    guess_one = (-near_left + 5.0 * centre + 2.0 * near_right) / 6.0
    guess_two = (2.0 * centre + 5.0 * near_right - far_right) / 6.0
    return (weight_zero * guess_zero + weight_one * guess_one + weight_two * guess_two) / (weight_zero + weight_one + weight_two)


def flux_difference(extended, speed_ext, axis, length):
    faces = length + 1

    def window(array, start, count):
        return lax.slice_in_dim(array, start, start + count, axis=axis)

    flux = speed_ext * extended
    magnitude = jnp.abs(speed_ext)
    face_speed = jnp.maximum(window(magnitude, 2, faces), window(magnitude, 3, faces))

    def upper(offset):
        return 0.5 * (window(flux, offset, faces) + face_speed * window(extended, offset, faces))

    def lower(offset):
        return 0.5 * (window(flux, offset, faces) - face_speed * window(extended, offset, faces))

    face_flux = weno_face(upper(0), upper(1), upper(2), upper(3), upper(4)) + weno_face(lower(5), lower(4), lower(3), lower(2), lower(1))
    return window(face_flux, 1, length) - window(face_flux, 0, length)


def wrap_pad(field, axis):
    length = field.shape[axis]
    return jnp.concatenate([lax.slice_in_dim(field, length - 3, length, axis=axis), field, lax.slice_in_dim(field, 0, 3, axis=axis)], axis=axis)


def transport(state, velocity):
    def per_variable(single):
        single = single[None]
        total = flux_difference(wrap_pad(single, 1), wrap_pad(velocity[0:1], 1), 1, single.shape[1])
        total = total + flux_difference(wrap_pad(single, 2), wrap_pad(velocity[1:2], 2), 2, single.shape[2])
        total = total + flux_difference(wrap_pad(single, 3), wrap_pad(velocity[2:3], 3), 3, single.shape[3])
        return -total[0]

    return lax.map(per_variable, state)


def to_blocks(field):
    channels, size_x, size_y, size_z = field.shape
    shaped = field.reshape(channels, size_x // BS, BS, size_y // BS, BS, size_z // BS, BS)
    shaped = shaped.transpose(1, 3, 5, 0, 2, 4, 6)
    return shaped.reshape(-1, channels, BS ** 3)


def from_blocks(blocks, size_x, size_y, size_z):
    channels = blocks.shape[1]
    shaped = blocks.reshape(size_x // BS, size_y // BS, size_z // BS, channels, BS, BS, BS)
    shaped = shaped.transpose(3, 0, 4, 1, 5, 2, 6)
    return shaped.reshape(channels, size_x, size_y, size_z)


def closure_block(features, w_in, w_mid, w_deep, w_out):
    hidden = jax.nn.silu(jnp.dot(w_in, features, preferred_element_type=jnp.float32)).astype(jnp.bfloat16)
    hidden = jax.nn.silu(jnp.dot(w_mid, hidden, preferred_element_type=jnp.float32)).astype(jnp.bfloat16)
    hidden = jax.nn.silu(jnp.dot(w_deep, hidden, preferred_element_type=jnp.float32)).astype(jnp.bfloat16)
    return jnp.dot(w_out, hidden, preferred_element_type=jnp.float32)


def sources(state, velocity, routes, w_in, w_mid, w_deep, w_out):
    features = jnp.concatenate([to_blocks(state), to_blocks(velocity)], axis=1).astype(jnp.bfloat16)
    band_flat = (routes.reshape(-1) >= 0).astype(jnp.int32)
    picked = jnp.nonzero(band_flat, size=NBAND)[0].astype(jnp.int32)

    def evaluate(block_index):
        return closure_block(features[block_index], w_in, w_mid, w_deep, w_out)

    evaluated = lax.map(evaluate, picked)
    blocks = jnp.zeros((band_flat.shape[0], state.shape[0], BS ** 3), jnp.float32).at[picked].set(evaluated)
    return from_blocks(blocks, state.shape[1], state.shape[2], state.shape[3])


def reference(state, velocity, routes, w_in, w_mid, w_deep, w_out):
    def rate(field):
        return transport(field, velocity) + sources(field, velocity, routes, w_in, w_mid, w_deep, w_out)

    first = state + STEP * rate(state)
    return 0.75 * state + 0.25 * (first + STEP * rate(first))
```

```python
import functools

import jax
import jax.numpy as jnp
from jax import lax
from jax.experimental import pallas as pl
from jax.experimental.pallas import tpu as pltpu
from jax.sharding import PartitionSpec as P

BS = 16
EPS = 1e-06
STEP = 0.25
NV = 4
NF = 7
HID = 128
WENO_TYPE = jnp.float32
SILU_TYPE = jnp.float32
VMEM_LIMIT = 56 * 1024 * 1024


def curvature(d1, d2, d3, d4):
    one = lambda x: jnp.asarray(x, d1.dtype)
    g2 = one(0.609375) * (d2 * d2) + one(0.75 * EPS)
    g3 = one(0.609375) * (d3 * d3) + one(0.75 * EPS)
    e0 = d1 - one(1.375) * d2
    e1 = d2 - one(0.625) * d3
    e2 = d4 - one(1.375) * d3
    r0 = reciprocal(e0 * e0 + g2)
    r1 = reciprocal(e1 * e1 + g3)
    r2 = reciprocal(e2 * e2 + g3)
    s1 = d3 - d2
    t0 = s1 - (d2 - d1)
    t2 = (d4 - d3) - s1
    w0 = r0 * r0
    w2 = one(1.5) * (r2 * r2)
    total = one(0.5) * w0 + one(3.0) * (r1 * r1) + w2
    return (w0 * t0 + w2 * t2) * reciprocal(total)


def reciprocal(x):
    return pl.reciprocal(x, approx=True)


def face_flux(fd, vd, alpha, centre):
    m = [alpha * d for d in vd]
    p = [(fd[j] + m[j]).astype(WENO_TYPE) for j in range(4)]
    q = [(fd[j] - m[j]).astype(WENO_TYPE) for j in range(1, 5)]
    bend = (curvature(*p) - curvature(*q[::-1])).astype(jnp.float32)
    rest = (fd[1] - fd[3]) + ((m[1] - m[2]) + (m[3] - m[2])) - bend
    return centre + rest * (1.0 / 6.0)


def roll(x, shift):
    return pltpu.roll(x, shift % x.shape[-1], axis=x.ndim - 1)


def depth_kernel(s_ref, v_ref, band_ref, wsel_ref, wmid_ref, wdeep_ref, wout_ref, out_ref):
    nx, ny = s_ref.shape[1], s_ref.shape[2]
    do_closure(s_ref, v_ref, band_ref, wsel_ref, wmid_ref, wdeep_ref, wout_ref, out_ref)
    tiles = ny // 8

    @pl.loop(0, nx * tiles)
    def _(step):
        i = step // tiles
        y = pl.ds(pl.multiple_of((step % tiles) * 8, 8), 8)
        u = 0.5 * v_ref[2, i, y, :]
        mag = jnp.abs(u)
        alpha = jnp.maximum(mag, roll(mag, -1))
        for k in range(NV):
            v = s_ref[k, i, y, :]
            f = u * v
            f1 = roll(f, -1)
            fd = f1 - f
            vd = roll(v, -1) - v
            fds = [roll(fd, 2), roll(fd, 1), fd, roll(fd, -1), roll(fd, -2)]
            vds = [roll(vd, 2), roll(vd, 1), vd, roll(vd, -1), roll(vd, -2)]
            flux = face_flux(fds, vds, alpha, f + f1)
            out_ref[k, i, y, :] = out_ref[k, i, y, :] - (flux - roll(flux, 1))


GX = 4


def silu_half(h):
    h = h.astype(SILU_TYPE)
    return (h + h * jnp.tanh(h)).astype(jnp.bfloat16)


def do_closure(s_ref, v_ref, band_ref, wsel_ref, wmid_ref, wdeep_ref, wout_ref, out_ref):
    nx, ny, nz = s_ref.shape[1:]
    rows = ny // BS

    @pl.loop(0, (nx // GX) * rows)
    def _(step):
        i0 = (step // rows) * GX
        y = pl.ds(pl.multiple_of((step % rows) * BS, BS), BS)
        feats = []
        for g in range(GX):
            parts = [s_ref[k, i0 + g, y, :].astype(jnp.bfloat16) for k in range(NV)]
            parts += [v_ref[k, i0 + g, y, :].astype(jnp.bfloat16) for k in range(3)]
            parts.append(jnp.zeros_like(parts[0]))
            feats.append(jnp.concatenate(parts, axis=0).T)
        lhs = jnp.concatenate(feats, axis=0)
        total = jnp.zeros((GX * nz, 128), jnp.float32)
        for p in range(BS // 2):
            h = jnp.dot(lhs, wsel_ref[:, p * 256:(p + 1) * 256], preferred_element_type=jnp.float32)
            h = silu_half(h)
            h = silu_half(jnp.dot(h, wmid_ref[...], preferred_element_type=jnp.float32))
            h = silu_half(jnp.dot(h, wdeep_ref[...], preferred_element_type=jnp.float32))
            total = total + jnp.dot(h, wout_ref[p * 256:(p + 1) * 256, :], preferred_element_type=jnp.float32)
        band = band_ref[i0 // BS, step % rows, :]
        for g in range(GX):
            back = total[g * nz:(g + 1) * nz].T
            for k in range(NV):
                out_ref[k, i0 + g, y, :] = jnp.where(band[None, :] > 0, back[k * BS:(k + 1) * BS, :], 0.0)


def cross_kernel(last, *refs):
    if last:
        s_ref, v_ref, r_ref, xlo, xhi, ylo, yhi, uxlo, uxhi, uylo, uyhi, old_ref, out_ref, acc = refs
    else:
        s_ref, v_ref, r_ref, xlo, xhi, ylo, yhi, uxlo, uxhi, uylo, uyhi, out_ref, acc = refs
    nx, ny = s_ref.shape[1], s_ref.shape[2]

    def sweep(n, load_v, load_u, emit):
        u_prev, v_prev = None, None
        fds, vds, us, fs = [], [], [], []
        prev_flux = None
        mags = []
        for j in range(-3, n + 3):
            u = 0.5 * load_u(j)
            v = load_v(j)
            f = u * v
            us.append(u)
            fs.append(f)
            if v_prev is not None:
                fds.append(f - fs[-2])
                vds.append(v - v_prev)
            v_prev = v
            if len(fds) >= 5:
                i = len(us) - 1
                alpha = jnp.maximum(jnp.abs(us[i - 3]), jnp.abs(us[i - 2]))
                flux = face_flux(fds[-5:], vds[-5:], alpha, fs[i - 3] + fs[i - 2])
                if prev_flux is not None:
                    emit(j - 3, flux - prev_flux)
                prev_flux = flux

    ytiles = ny // 8
    xtiles = nx // 8

    @pl.loop(0, xtiles * NV)
    def _(step):
        k = step // xtiles
        x0 = pl.multiple_of((step % xtiles) * 8, 8)
        xs = pl.ds(x0, 8)

        def load_v(j):
            if j < 0:
                return ylo[k, j + 3, xs, :].astype(jnp.float32)
            if j >= ny:
                return yhi[k, j - ny, xs, :].astype(jnp.float32)
            return s_ref.reshape(NV * nx * ny, 128)[pl.ds((k * nx + x0) * ny + j, 8, stride=ny), :]

        def load_u(j):
            if j < 0:
                return uylo[j + 3, xs, :].astype(jnp.float32)
            if j >= ny:
                return uyhi[j - ny, xs, :].astype(jnp.float32)
            return v_ref.reshape(3 * nx * ny, 128)[pl.ds((nx + x0) * ny + j, 8, stride=ny), :]

        def emit(j, value):
            acc.reshape(NV * nx * ny, 128)[pl.ds((k * nx + x0) * ny + j, 8, stride=ny), :] = value

        sweep(ny, load_v, load_u, emit)

    @pl.loop(0, ytiles * NV)
    def _(step):
        k = step // ytiles
        ys = pl.ds(pl.multiple_of((step % ytiles) * 8, 8), 8)

        def load_v(j):
            if j < 0:
                return xlo[k, j + 3, ys, :].astype(jnp.float32)
            if j >= nx:
                return xhi[k, j - nx, ys, :].astype(jnp.float32)
            return s_ref[k, j, ys, :]

        def load_u(j):
            if j < 0:
                return uxlo[j + 3, ys, :].astype(jnp.float32)
            if j >= nx:
                return uxhi[j - nx, ys, :].astype(jnp.float32)
            return v_ref[0, j, ys, :]

        def emit(j, value):
            rate = r_ref[k, j, ys, :] - acc[k, j, ys, :] - value
            stepped = s_ref[k, j, ys, :] + STEP * rate
            if last:
                stepped = 0.75 * old_ref[k, j, ys, :] + 0.25 * stepped
            out_ref[k, j, ys, :] = stepped

        sweep(nx, load_v, load_u, emit)


def vmem(n):
    return [pl.BlockSpec(memory_space=pltpu.VMEM)] * n


def depth_call(state, velocity, band, weights):
    cells = state.size // NV
    return pl.pallas_call(
        depth_kernel,
        out_shape=jax.ShapeDtypeStruct(state.shape, jnp.float32),
        in_specs=vmem(7),
        out_specs=pl.BlockSpec(memory_space=pltpu.VMEM),
        compiler_params=pltpu.CompilerParams(vmem_limit_bytes=VMEM_LIMIT),
        cost_estimate=pl.CostEstimate(flops=cells * 262144, bytes_accessed=6 << 20, transcendentals=0),
        name="depth",
    )(state, velocity, band, *weights)


def cross_call(state, velocity, part, halos, old):
    last = old is not None
    args = (state, velocity, part, *halos) + ((old,) if last else ())
    return pl.pallas_call(
        functools.partial(cross_kernel, last),
        out_shape=jax.ShapeDtypeStruct(state.shape, jnp.float32),
        in_specs=vmem(len(args)),
        out_specs=pl.BlockSpec(memory_space=pltpu.VMEM),
        scratch_shapes=[pltpu.VMEM(state.shape, jnp.float32)],
        compiler_params=pltpu.CompilerParams(vmem_limit_bytes=VMEM_LIMIT),
        name="cross",
    )(*args)


def send(value, axis, up):
    n = lax.axis_size(axis)
    if up:
        return lax.ppermute(value, axis, [(i, (i + 1) % n) for i in range(n)])
    return lax.ppermute(value, axis, [((i + 1) % n, i) for i in range(n)])


def halos_of(field):
    small = field.astype(jnp.bfloat16)
    xlo = send(small[:, -3:], "gx", True)
    xhi = send(small[:, :3], "gx", False)
    ylo = send(small[:, :, -3:].transpose(0, 2, 1, 3), "gy", True)
    yhi = send(small[:, :, :3].transpose(0, 2, 1, 3), "gy", False)
    return xlo, xhi, ylo, yhi


def prepare(w_in, w_mid, w_deep, w_out):
    half = jnp.asarray(0.5, jnp.bfloat16)
    eye = jnp.eye(BS, dtype=jnp.bfloat16)
    padded = jnp.pad(w_in.T * half, ((0, 1), (0, 0)))
    wsel = (padded[:, None, None, :] * eye[None, :, :, None]).reshape(8 * BS, BS * HID)
    two = jnp.eye(2, dtype=jnp.bfloat16)
    wmid = jnp.kron(two, w_mid.T * half)
    wdeep = jnp.kron(two, w_deep.T * half)
    wout = (w_out.T[None, :, :, None] * eye[:, None, None, :]).reshape(BS * HID, NV * BS)
    wout = jnp.pad(wout, ((0, 0), (0, 128 - NV * BS)))
    return wsel, wmid, wdeep, wout


def shards(state, velocity, routes, w_in, w_mid, w_deep, w_out):
    weights = prepare(w_in, w_mid, w_deep, w_out)
    band = jnp.repeat((routes >= 0).astype(jnp.float32), BS, axis=2)
    vx = velocity[0].astype(jnp.bfloat16)
    vy = velocity[1].astype(jnp.bfloat16)
    speeds = (
        send(vx[-3:], "gx", True),
        send(vx[:3], "gx", False),
        send(vy[:, -3:].transpose(1, 0, 2), "gy", True),
        send(vy[:, :3].transpose(1, 0, 2), "gy", False),
    )

    halos = halos_of(state) + speeds
    part = depth_call(state, velocity, band, weights)
    first = cross_call(state, velocity, part, halos, None)
    halos = halos_of(first) + speeds
    part = depth_call(first, velocity, band, weights)
    return cross_call(first, velocity, part, halos, state)


def solution(mesh):
    placed = (
        P(None, "gx", "gy", None),
        P(None, "gx", "gy", None),
        P("gx", "gy", None),
        P(),
        P(),
        P(),
        P(),
    )
    return jax.shard_map(
        shards, mesh=mesh, in_specs=placed, out_specs=P(None, "gx", "gy", None), check_vma=False
    )
```

```python
import functools

import jax
import jax.numpy as jnp
from jax import lax
from jax.experimental import pallas as pl
from jax.experimental.pallas import tpu as pltpu
from jax.sharding import PartitionSpec as P

BS = 16
EPS = 1e-06
STEP = 0.25
NV = 4
NF = 7
HID = 128
PAIRS = 16
CHUNK = 8
EARLY = 8
WENO_TYPE = jnp.float32
SILU_TYPE = jnp.bfloat16
VMEM_LIMIT = 60 * 1024 * 1024


def reciprocal(x):
    return pl.reciprocal(x, approx=True)


def curvature(d1, d2, d3, d4):
    one = lambda x: jnp.asarray(x, d1.dtype)
    g2 = one(0.609375) * (d2 * d2) + one(0.75 * EPS)
    g3 = one(0.609375) * (d3 * d3) + one(0.75 * EPS)
    e0 = d1 - one(1.375) * d2
    e1 = d2 - one(0.625) * d3
    e2 = d4 - one(1.375) * d3
    r0 = reciprocal(e0 * e0 + g2)
    r1 = reciprocal(e1 * e1 + g3)
    r2 = reciprocal(e2 * e2 + g3)
    s1 = d3 - d2
    t0 = s1 - (d2 - d1)
    t2 = (d4 - d3) - s1
    w0 = r0 * r0
    w2 = one(1.5) * (r2 * r2)
    total = one(0.5) * w0 + one(3.0) * (r1 * r1) + w2
    return (w0 * t0 + w2 * t2) * reciprocal(total)


def face_flux(fd, vd, alpha, centre):
    m = [alpha * d for d in vd]
    p = [(fd[j] + m[j]).astype(WENO_TYPE) for j in range(4)]
    q = [(fd[j] - m[j]).astype(WENO_TYPE) for j in range(1, 5)]
    bend = (curvature(*p) - curvature(*q[::-1])).astype(jnp.float32)
    rest = (fd[1] - fd[3]) + ((m[1] - m[2]) + (m[3] - m[2])) - bend
    return centre + rest * (1.0 / 6.0)


def sweep(n, load_v, load_u, emit):
    vs, us, fs, fds, vds = [], [], [], [], []
    previous = None
    for j in range(-3, n + 3):
        u, v = load_u(j), load_v(j)
        us.append(u)
        vs.append(v)
        fs.append(u * v)
        if len(vs) > 1:
            fds.append(fs[-1] - fs[-2])
            vds.append(vs[-1] - vs[-2])
        if len(fds) >= 5:
            alpha = jnp.maximum(jnp.abs(us[-4]), jnp.abs(us[-3]))
            flux = face_flux(fds[-5:], vds[-5:], alpha, fs[-4] + fs[-3])
            if previous is not None:
                emit(j - 3, flux - previous)
            previous = flux
        yield


def silu_half(h):
    h = h.astype(SILU_TYPE)
    return (h + h * jnp.tanh(h)).astype(jnp.bfloat16)


def closure_part(pair, planes, st_ref, vt_ref, weights, tot_ref):
    wsel_ref, wmid_ref, wdeep_ref, wout_ref = weights
    for lo in range(planes[0], planes[1], CHUNK):
        size = min(CHUNK, planes[1] - lo)
        rows = size * 128
        span = pl.ds(lo, size)
        lhs = jnp.concatenate([st_ref[span].reshape(rows, 128), vt_ref[span].reshape(rows, 128)], axis=1)
        h = silu_half(jnp.dot(lhs, wsel_ref[pair], preferred_element_type=jnp.float32))
        yield
        h = silu_half(jnp.dot(h, wmid_ref[...], preferred_element_type=jnp.float32))
        yield
        h = silu_half(jnp.dot(h, wdeep_ref[...], preferred_element_type=jnp.float32))
        yield
        out = jnp.dot(h, wout_ref[pair], preferred_element_type=jnp.float32)
        tot_ref[span] = tot_ref[span] + out.reshape(size, 128, 128)
        yield


def together(*parts):
    done = [0] * len(parts)
    while any(d < n for d, (_, n) in zip(done, parts)):
        i = min(range(len(parts)), key=lambda a: (done[a] + 0.5) / parts[a][1] if done[a] < parts[a][1] else 9.0)
        next(parts[i][0], None)
        done[i] += 1
    for gen, _ in parts:
        for _ in gen:
            pass


def depth_kernel(opening, *refs):
    if opening:
        s_ref, v_ref, band_ref, *weights = refs[:7]
        rt_ref, stb_ref, vtb_ref, ut_ref, st, tot = refs[7:]
    else:
        s_ref, vtb_ref, ut_ref, band_ref, *weights = refs[:8]
        rt_ref, stb_ref, st, tot = refs[8:]
    nx, ny = s_ref.shape[1], s_ref.shape[2]

    @pl.loop(0, nx, unroll=2)
    def _(x):
        t = jnp.concatenate([s_ref[k, x] for k in range(NV)], axis=0).T
        st[x] = t
        stb_ref[x] = t.astype(jnp.bfloat16)
        if opening:
            w = v_ref[2, x]
            vt = jnp.concatenate([v_ref[0, x], v_ref[1, x], w, jnp.zeros_like(w)], axis=0).T
            vtb_ref[x] = vt.astype(jnp.bfloat16)
            ut_ref[x] = jnp.concatenate([0.5 * w] * NV, axis=0).T

    @pl.loop(0, EARLY)
    def _(x):
        tot[x] = jnp.zeros((128, 128), jnp.float32)

    st2 = st.reshape(nx * 128, 128)
    ut2 = ut_ref.reshape(nx * 128, 128)
    rt2 = rt_ref.reshape(nx * 128, 128)

    @pl.loop(0, PAIRS)
    def _(step):
        x0 = (step // 4) * 8
        z0 = (step % 4) * 32

        def at(j):
            return pl.ds(x0 * 128 + ((z0 + j) & 127), 8, stride=128)

        def emit(j, value):
            rt2[at(j), :] = -value

        column = sweep(32, lambda j: st2[at(j), :], lambda j: ut2[at(j), :], emit)
        closure = closure_part(step, (0, EARLY), stb_ref, vtb_ref, weights, tot)
        together((closure, -(-EARLY // CHUNK) * 4), (column, 38))

    @pl.loop(0, EARLY)
    def _(x):
        rt_ref[x] = rt_ref[x] + jnp.where(band_ref[x // BS] > 0, tot[x], 0.0)


def cross_kernel(last, *refs):
    s_ref, v_ref, rt_ref, stb_ref, vtb_ref, band_ref, *weights = refs[:10]
    xlo, xhi, ylo, yhi, uxlo, uxhi, uylo, uyhi = refs[10:18]
    if last:
        old_ref, out_ref, dx, dy, tot = refs[18:]
    else:
        out_ref, *slabs = refs[18:23]
        dx, dy, tot = refs[23:]
    nx, ny = s_ref.shape[1], s_ref.shape[2]
    s2 = s_ref.reshape(NV * nx * ny, 128)
    v2 = v_ref.reshape(3 * nx * ny, 128)
    dy2 = dy.reshape(NV * nx * ny, 128)

    @pl.loop(EARLY, nx)
    def _(x):
        tot[x] = jnp.zeros((128, 128), jnp.float32)

    @pl.loop(0, PAIRS)
    def _(step):
        k = step // 4
        c0 = pl.multiple_of((step % 4) * 8, 8)
        cs = pl.ds(c0, 8)

        def wide(ref, *index):
            return ref[(*index, cs, slice(None))].astype(jnp.float32)

        def yv(j):
            if j < 0:
                return wide(ylo, k, j + 3)
            if j >= ny:
                return wide(yhi, k, j - ny)
            return s2[pl.ds((k * nx + c0) * ny + j, 8, stride=ny), :]

        def yu(j):
            if j < 0:
                return 0.5 * wide(uylo, j + 3)
            if j >= ny:
                return 0.5 * wide(uyhi, j - ny)
            return 0.5 * v2[pl.ds((nx + c0) * ny + j, 8, stride=ny), :]

        def yemit(j, value):
            dy2[pl.ds((k * nx + c0) * ny + j, 8, stride=ny), :] = value

        def xv(j):
            if j < 0:
                return wide(xlo, k, j + 3)
            if j >= nx:
                return wide(xhi, k, j - nx)
            return s_ref[k, j, cs, :]

        def xu(j):
            if j < 0:
                return 0.5 * wide(uxlo, j + 3)
            if j >= nx:
                return 0.5 * wide(uxhi, j - nx)
            return 0.5 * v_ref[0, j, cs, :]

        def xemit(j, value):
            dx[k, j, cs, :] = value

        closure = closure_part(step, (EARLY, nx), stb_ref, vtb_ref, weights, tot)
        together(
            (closure, -(-(nx - EARLY) // CHUNK) * 4),
            (sweep(ny, yv, yu, yemit), ny + 6),
            (sweep(nx, xv, xu, xemit), nx + 6),
        )

    def finish(x, rate_t):
        back = rate_t.T
        for k in range(NV):
            rate = back[k * ny : (k + 1) * ny] - (dx[k, x] + dy[k, x])
            stepped = s_ref[k, x] + STEP * rate
            if last:
                stepped = 0.75 * old_ref[k, x] + 0.25 * stepped
            out_ref[k, x] = stepped

    @pl.loop(0, EARLY)
    def _(x):
        finish(x, rt_ref[x])

    @pl.loop(EARLY, nx)
    def _(x):
        finish(x, rt_ref[x] + jnp.where(band_ref[x // BS] > 0, tot[x], 0.0))

    if not last:
        cut_slabs(out_ref, [(k, k) for k in range(NV)], *slabs)


def cut_slabs(ref, which, to_lo_x, to_hi_x, to_lo_y, to_hi_y):
    lead, nx, ny = ref.shape[:3]
    flat = ref.reshape(lead * nx * ny, 128)
    for src, dst in which:
        for j in range(3):
            to_lo_x[dst, j] = ref[src, j].astype(jnp.bfloat16)
            to_hi_x[dst, j] = ref[src, nx - 3 + j].astype(jnp.bfloat16)
            for target, y in ((to_lo_y, j), (to_hi_y, ny - 3 + j)):
                target[dst, j] = flat[pl.ds(src * nx * ny + y, nx, stride=ny), :].astype(jnp.bfloat16)


def slab_kernel(s_ref, v_ref, *slabs):
    cut_slabs(s_ref, [(k, k) for k in range(NV)], *slabs)
    nx, ny = v_ref.shape[1], v_ref.shape[2]
    flat = v_ref.reshape(3 * nx * ny, 128)
    for j in range(3):
        slabs[0][NV, j] = v_ref[0, j].astype(jnp.bfloat16)
        slabs[1][NV, j] = v_ref[0, nx - 3 + j].astype(jnp.bfloat16)
        slabs[2][NV, j] = flat[pl.ds(nx * ny + j, nx, stride=ny), :].astype(jnp.bfloat16)
        slabs[3][NV, j] = flat[pl.ds(nx * ny + ny - 3 + j, nx, stride=ny), :].astype(jnp.bfloat16)


VM = pl.BlockSpec(memory_space=pltpu.VMEM)
PARAMS = pltpu.CompilerParams(vmem_limit_bytes=VMEM_LIMIT)


def slab_shapes(count, n):
    return [jax.ShapeDtypeStruct((count, 3, n, 128), jnp.bfloat16)] * 4


def slab_call(state, velocity):
    n = state.shape[1]
    return pl.pallas_call(
        slab_kernel,
        out_shape=slab_shapes(NV + 1, n),
        in_specs=[VM] * 2,
        out_specs=[VM] * 4,
        compiler_params=PARAMS,
        name="slabs",
    )(state, velocity)


def depth_call(opening, state, extra, band, weights):
    n = state.shape[1]
    plane = lambda dtype: jax.ShapeDtypeStruct((n, 128, 128), dtype)
    shapes = [plane(jnp.float32), plane(jnp.bfloat16)]
    if opening:
        shapes += [plane(jnp.bfloat16), plane(jnp.float32)]
    args = (state, *extra, band, *weights)
    return pl.pallas_call(
        functools.partial(depth_kernel, opening),
        out_shape=shapes,
        in_specs=[VM] * len(args),
        out_specs=[VM] * len(shapes),
        scratch_shapes=[pltpu.VMEM((n, 128, 128), jnp.float32), pltpu.VMEM((EARLY, 128, 128), jnp.float32)],
        compiler_params=PARAMS,
        cost_estimate=pl.CostEstimate(flops=1 << 34, bytes_accessed=8 << 20, transcendentals=0),
        name="depth",
    )(*args)


def cross_call(state, velocity, parts, band, weights, halos, old):
    n = state.shape[1]
    last = old is not None
    args = (state, velocity, *parts, band, *weights, *halos) + ((old,) if last else ())
    shapes = [jax.ShapeDtypeStruct(state.shape, jnp.float32)]
    if not last:
        shapes += slab_shapes(NV, n)
    return pl.pallas_call(
        functools.partial(cross_kernel, last),
        out_shape=shapes,
        in_specs=[VM] * len(args),
        out_specs=[VM] * len(shapes),
        scratch_shapes=[pltpu.VMEM(state.shape, jnp.float32)] * 2 + [pltpu.VMEM((n, 128, 128), jnp.float32)],
        compiler_params=PARAMS,
        cost_estimate=pl.CostEstimate(flops=1 << 35, bytes_accessed=12 << 20, transcendentals=0),
        name="cross",
    )(*args)


def send(value, axis, up):
    n = lax.axis_size(axis)
    if up:
        return lax.ppermute(value, axis, [(i, (i + 1) % n) for i in range(n)])
    return lax.ppermute(value, axis, [((i + 1) % n, i) for i in range(n)])


def exchange(to_lo_x, to_hi_x, to_lo_y, to_hi_y):
    return [
        send(to_hi_x, "gx", True),
        send(to_lo_x, "gx", False),
        send(to_hi_y, "gy", True),
        send(to_lo_y, "gy", False),
    ]


def prepare(w_in, w_mid, w_deep, w_out, ny):
    half = jnp.asarray(0.5, jnp.bfloat16)
    zero = jnp.asarray(0.0, jnp.bfloat16)
    two = jnp.eye(2, dtype=jnp.bfloat16)
    wide = jnp.tile(jnp.pad(w_in.T * half, ((0, 1), (0, 0))), (1, 2))
    shape = (PAIRS, 8, ny, 2 * HID)
    row = 2 * lax.broadcasted_iota(jnp.int32, shape, 0) + lax.broadcasted_iota(jnp.int32, shape, 3) // HID
    hit = row == lax.broadcasted_iota(jnp.int32, shape, 2)
    wsel = jnp.where(hit, wide[None, :, None, :], zero).reshape(PAIRS, 8 * ny, 2 * HID)
    wmid = jnp.kron(two, w_mid.T * half)
    wdeep = jnp.kron(two, w_deep.T * half)
    shape = (PAIRS, 2 * HID, NV * ny)
    row = 2 * lax.broadcasted_iota(jnp.int32, shape, 0) + lax.broadcasted_iota(jnp.int32, shape, 1) // HID
    hit = row == lax.broadcasted_iota(jnp.int32, shape, 2) % ny
    wout = jnp.where(hit, jnp.tile(jnp.repeat(w_out.T, ny, axis=1), (2, 1))[None], zero)
    return wsel, wmid, wdeep, wout


def shards(state, velocity, routes, w_in, w_mid, w_deep, w_out):
    ny = state.shape[2]
    cut = slab_call(state, velocity)
    halos = exchange(*cut)
    speeds = [h[NV] for h in halos]
    weights = prepare(w_in, w_mid, w_deep, w_out, ny)
    member = (routes >= 0).astype(jnp.float32)
    band = jnp.repeat(member.transpose(0, 2, 1), BS, axis=1)
    band = jnp.tile(jnp.repeat(band, BS, axis=2), (1, 1, NV))

    rt, stb, vtb, ut = depth_call(True, state, (velocity,), band, weights)
    first, *cut = cross_call(state, velocity, (rt, stb, vtb), band, weights, halos + speeds, None)
    halos = exchange(*cut)
    rt, stb = depth_call(False, first, (vtb, ut), band, weights)
    return cross_call(first, velocity, (rt, stb, vtb), band, weights, halos + speeds, state)[0]


def solution(mesh):
    placed = (
        P(None, "gx", "gy", None),
        P(None, "gx", "gy", None),
        P("gx", "gy", None),
        P(),
        P(),
        P(),
        P(),
    )
    return jax.shard_map(
        shards, mesh=mesh, in_specs=placed, out_specs=P(None, "gx", "gy", None), check_vma=False
    )
```

```python
import functools

import jax
import jax.numpy as jnp
from jax import lax
from jax.experimental import pallas as pl
from jax.experimental.pallas import tpu as pltpu
from jax.sharding import PartitionSpec as P

BS = 16
EPS = 1e-06
STEP = 0.25
NV = 4
NF = 7
HID = 128
PAIRS = 16
DEPTH_SIZE = 4
CROSS_SIZE = 8
EARLY = 8
WENO_TYPE = jnp.bfloat16
SILU_TYPE = jnp.bfloat16
TILE = 16
VMEM_LIMIT = 60 * 1024 * 1024


def reciprocal(x):
    return pl.reciprocal(x, approx=True)


def curvature(d1, d2, d3, d4):
    one = lambda x: jnp.asarray(x, d1.dtype)
    g2 = one(0.609375) * (d2 * d2) + one(0.75 * EPS)
    g3 = one(0.609375) * (d3 * d3) + one(0.75 * EPS)
    e0 = d1 - one(1.375) * d2
    e1 = d3 - one(0.625) * d2
    e2 = d4 - one(1.375) * d3
    r0 = reciprocal(e0 * e0 + g2)
    r1 = reciprocal(e1 * e1 + g2)
    r2 = reciprocal(e2 * e2 + g3)
    t0 = e0 + e1
    t2 = e2 + (d2 - one(0.625) * d3)
    w0 = r0 * r0
    w2 = one(1.5) * (r2 * r2)
    total = one(0.5) * w0 + one(3.0) * (r1 * r1) + w2
    return (w0 * t0 + w2 * t2) * reciprocal(total)


def face_flux(fd, vd, second, alpha, centre):
    rough = alpha.astype(WENO_TYPE)
    m = [rough * d for d in vd]
    p = [fd[j] + m[j] for j in range(4)]
    q = [fd[j] - m[j] for j in range(1, 5)]
    bend = (curvature(*p) - curvature(*q[::-1])).astype(jnp.float32)
    before, after, v_before, v_after = second
    rest = (before - after) + alpha * (v_after - v_before) - bend
    return centre + rest * (1.0 / 6.0)


class Sweep:
    def __init__(self, n, load_v, load_u, emit):
        self.last, self.load_v, self.load_u, self.emit = n + 3, load_v, load_u, emit

    def points(self):
        return range(-3, self.last)

    def advance(self, state, j):
        us, fs, vs, fds, vds, frough, vrough, vseconds, before = state
        u, v = self.load_u(j), self.load_v(j)
        f = u * v
        if vs:
            fds = fds + [f - fs[-1]]
            vds = vds + [v - vs[-1]]
            frough = frough + [fds[-1].astype(WENO_TYPE)]
            vrough = vrough + [vds[-1].astype(WENO_TYPE)]
        if len(vds) > 1:
            vseconds = vseconds + [vds[-1] - vds[-2]]
        us, fs = us + [u], fs + [f]
        if len(frough) == 5:
            alpha = jnp.maximum(jnp.abs(us[0]), jnp.abs(us[1]))
            second = (fds[-4], fds[-2], vseconds[-3], vseconds[-2])
            flux = face_flux(frough, vrough, second, alpha, fs[0] + fs[1])
            if before:
                self.emit(j - 3, flux - before[0])
            before = [flux]
        return us[-3:], fs[-3:], [v], fds[-4:], vds[-1:], frough[-4:], vrough[-4:], vseconds[-3:], before


def silu_half(h):
    h = h.astype(SILU_TYPE)
    return (h + h * jnp.tanh(h)).astype(jnp.bfloat16)


def closure_part(pair, planes, size, st_ref, vt_ref, weights, tot_ref, hidden, keys, accs):
    wsel_ref, wmid_ref, wdeep_ref, wout_ref = weights
    chunks = (planes[1] - planes[0]) // size
    half = size * 64
    zero = jnp.zeros((2 * HID, 2 * HID), jnp.float32)
    layers = (
        lambda: jnp.where(keys[0] == 2 * pair, wsel_ref[...], zero).astype(jnp.bfloat16),
        lambda: wmid_ref[...],
        lambda: wdeep_ref[...],
        lambda: jnp.concatenate(
            [jnp.where(keys[1][:, :128] == 2 * pair, wout_ref[...], zero[:, :128]), zero[:, 128:]], axis=1
        ).astype(jnp.bfloat16),
    )
    waiting = None

    def push(layer):
        for m in range(2):
            pltpu.matmul_push_rhs(layers[layer](), layer % 2, m)

    def take(layer, c, r):
        for m in range(2):
            sums = pltpu.matmul_pop(accs[2 * m + r])
            if layer < 3:
                hidden[c, pl.ds(m * half, half), :] = silu_half(sums)
            else:
                span = pl.ds(planes[0] + c * size + m * size // 2, size // 2)
                tot_ref[span] = tot_ref[span] + sums[:, :128].reshape(size // 2, 128, 128)

    push(0)
    for layer in range(4):
        for c in range(chunks):
            r = (layer * chunks + c) % 2
            for m in range(2):
                if layer == 0:
                    span = pl.ds(planes[0] + c * size + m * size // 2, size // 2)
                    lhs = jnp.concatenate([st_ref[span].reshape(half, 128), vt_ref[span].reshape(half, 128)], axis=1)
                else:
                    lhs = hidden[c, pl.ds(m * half, half), :]
                pltpu.matmul_acc_lhs(accs[2 * m + r], lhs, layer % 2 if c == 0 else None)
            if c == 0 and layer < 3:
                push(layer + 1)
            if waiting is not None:
                take(*waiting)
            waiting = (layer, c, r)
            yield
    take(*waiting)
    yield


def together(closure, steps, sweeps):
    work = [(sweep, j) for sweep in sweeps for j in sweep.points()]
    costs = [1.0 if j > 1 else 0.15 for _, j in work]
    total, spent, at = sum(costs), 0.0, 0
    state, owner = None, None
    for i in range(steps):
        next(closure, None)
        while at < len(work) and (i == steps - 1 or spent + costs[at] / 2 < total * (i + 1) / steps):
            sweep, j = work[at]
            if sweep is not owner:
                state, owner = ([],) * 9, sweep
            state = sweep.advance(state, j)
            spent += costs[at]
            at += 1


def depth_kernel(opening, *refs):
    if opening:
        s_ref, v_ref, band_ref, *weights = refs[:7]
        rt_ref, stb_ref, vtb_ref, ut_ref, st, tot, hidden, keys = refs[7:]
    else:
        s_ref, vtb_ref, ut_ref, band_ref, *weights = refs[:8]
        rt_ref, stb_ref, st, tot, hidden, keys = refs[8:]
    nx, ny = s_ref.shape[1], s_ref.shape[2]

    @pl.loop(0, nx, unroll=4)
    def _(x):
        t = jnp.concatenate([s_ref[k, x] for k in range(NV)], axis=0).T
        st[x] = t
        stb_ref[x] = t.astype(jnp.bfloat16)
        if opening:
            w = v_ref[2, x]
            vt = jnp.concatenate([v_ref[0, x], v_ref[1, x], w, jnp.zeros_like(w)], axis=0).T
            vtb_ref[x] = vt.astype(jnp.bfloat16)
            ut_ref[x] = jnp.concatenate([0.5 * w] * NV, axis=0).T

    @pl.loop(0, EARLY, unroll=4)
    def _(x):
        tot[x] = jnp.zeros((128, 128), jnp.float32)

    st2 = st.reshape(nx * 128, 128)
    ut2 = ut_ref.reshape(nx * 128, 128)
    rt2 = rt_ref.reshape(nx * 128, 128)

    set_keys(keys)

    def main(*accs):
        @pl.loop(0, PAIRS)
        def _(step):
            x0 = (step // 8) * TILE
            z0 = (step % 8) * 16

            def at(j):
                return pl.ds(x0 * 128 + ((z0 + j) & 127), TILE, stride=128)

            def emit(j, value):
                rt2[at(j), :] = -value

            column = Sweep(16, lambda j: st2[at(j), :], lambda j: ut2[at(j), :], emit)
            closure = closure_part(step, (0, EARLY), DEPTH_SIZE, stb_ref, vtb_ref, weights, tot, hidden, keys, accs)
            together(closure, EARLY // DEPTH_SIZE * 4 + 1, (column,))

    with_sums(DEPTH_SIZE, main)

    @pl.loop(0, EARLY, unroll=4)
    def _(x):
        rt_ref[x] = rt_ref[x] + jnp.where(band_ref[x // BS] > 0, tot[x], 0.0)


def cross_kernel(last, *refs):
    s_ref, v_ref, rt_hbm, stb_ref, vtb_ref, band_ref, *weights = refs[:10]
    xlo, xhi, ylo, yhi = refs[10:14]
    rest = refs[14:] if not last else refs[18:]
    uxlo, uxhi, uylo, uyhi = (r.at[NV] for r in (refs[10:14] if not last else refs[14:18]))
    if last:
        old_hbm, out_hbm, dx, dy, tot, hidden, keys, rt_ref, out_ref, sems, old_ref = rest
    else:
        out_hbm, *slabs = rest[:5]
        dx, dy, tot, hidden, keys, rt_ref, out_ref, sems = rest[5:]
    nx, ny = s_ref.shape[1], s_ref.shape[2]
    s2 = s_ref.reshape(NV * nx * ny, 128)
    v2 = v_ref.reshape(3 * nx * ny, 128)
    dy2 = dy.reshape(NV * nx * ny, 128)
    coming = [pltpu.make_async_copy(rt_hbm, rt_ref, sems.at[0])]
    if last:
        coming.append(pltpu.make_async_copy(old_hbm, old_ref, sems.at[1]))
    for copy in coming:
        copy.start()

    @pl.loop(EARLY, nx, unroll=4)
    def _(x):
        tot[x] = jnp.zeros((128, 128), jnp.float32)

    set_keys(keys)

    def main(*accs):
        @pl.loop(0, PAIRS)
        def _(step):
            k = step // 4
            c0 = pl.multiple_of((step // 2 % 2) * TILE, TILE)
            cs = pl.ds(c0, TILE)
            base = (step % 2) * 16

            def wide(ref, *index):
                return ref[(*index, cs, slice(None))].astype(jnp.float32)

            def point(j, n, inner, lo, hi):
                if j < 0:
                    return jnp.where(base == 0, lo(j + 3), inner(jnp.maximum(base + j, 0)))
                if j >= 16:
                    return jnp.where(base == 0, inner(jnp.minimum(base + j, n - 1)), hi(j - 16))
                return inner(base + j)

            def column(lead, y):
                return pl.ds((lead * nx + c0) * ny + y, TILE, stride=ny)

            def yv(j):
                return point(j, ny, lambda y: s2[column(k, y), :], lambda i: wide(ylo, k, i), lambda i: wide(yhi, k, i))

            def yu(j):
                return 0.5 * point(j, ny, lambda y: v2[column(1, y), :], lambda i: wide(uylo, i), lambda i: wide(uyhi, i))

            def yemit(j, value):
                dy2[column(k, base + j), :] = value

            def xv(j):
                return point(j, nx, lambda x: s_ref[k, x, cs, :], lambda i: wide(xlo, k, i), lambda i: wide(xhi, k, i))

            def xu(j):
                return 0.5 * point(j, nx, lambda x: v_ref[0, x, cs, :], lambda i: wide(uxlo, i), lambda i: wide(uxhi, i))

            def xemit(j, value):
                dx[k, base + j, cs, :] = value

            closure = closure_part(step, (EARLY, nx), CROSS_SIZE, stb_ref, vtb_ref, weights, tot, hidden, keys, accs)
            together(
                closure,
                (nx - EARLY) // CROSS_SIZE * 4 + 1,
                (Sweep(16, yv, yu, yemit), Sweep(16, xv, xu, xemit)),
            )

    with_sums(CROSS_SIZE, main)

    def finish(x, rate_t):
        back = rate_t.T
        for k in range(NV):
            rate = back[k * ny : (k + 1) * ny] - (dx[k, x] + dy[k, x])
            stepped = s_ref[k, x] + STEP * rate
            if last:
                stepped = 0.75 * old_ref[k, x] + 0.25 * stepped
            out_ref[k, x] = stepped

    for copy in coming:
        copy.wait()
    going = []
    for part in range(4):
        lo, hi = part * nx // 4, (part + 1) * nx // 4

        @pl.loop(lo, hi, unroll=4)
        def _(x):
            rate_t = rt_ref[x]
            if lo >= EARLY:
                rate_t = rate_t + jnp.where(band_ref[x // BS] > 0, tot[x], 0.0)
            finish(x, rate_t)

        for k in range(NV):
            span = pl.ds(lo, hi - lo)
            going.append(pltpu.make_async_copy(out_ref.at[k, span], out_hbm.at[k, span], sems.at[2 + part * NV + k]))
            going[-1].start()

    if not last:
        cut_slabs(out_ref, [(k, k) for k in range(NV)], *slabs)
    for copy in going:
        copy.wait()


def cut_slabs(ref, which, to_lo_x, to_hi_x, to_lo_y, to_hi_y):
    lead, nx, ny = ref.shape[:3]
    flat = ref.reshape(lead * nx * ny, 128)
    for src, dst in which:
        for j in range(3):
            to_lo_x[dst, j] = ref[src, j].astype(jnp.bfloat16)
            to_hi_x[dst, j] = ref[src, nx - 3 + j].astype(jnp.bfloat16)
            for target, y in ((to_lo_y, j), (to_hi_y, ny - 3 + j)):
                target[dst, j] = flat[pl.ds(src * nx * ny + y, nx, stride=ny), :].astype(jnp.bfloat16)


def slab_kernel(s_ref, v_ref, *slabs):
    cut_slabs(s_ref, [(k, k) for k in range(NV)], *slabs)
    nx, ny = v_ref.shape[1], v_ref.shape[2]
    flat = v_ref.reshape(3 * nx * ny, 128)
    for j in range(3):
        slabs[0][NV, j] = v_ref[0, j].astype(jnp.bfloat16)
        slabs[1][NV, j] = v_ref[0, nx - 3 + j].astype(jnp.bfloat16)
        slabs[2][NV, j] = flat[pl.ds(nx * ny + j, nx, stride=ny), :].astype(jnp.bfloat16)
        slabs[3][NV, j] = flat[pl.ds(nx * ny + ny - 3 + j, nx, stride=ny), :].astype(jnp.bfloat16)


VM = pl.BlockSpec(memory_space=pltpu.VMEM)
ANY = pl.BlockSpec(memory_space=pl.ANY)
PARAMS = pltpu.CompilerParams(vmem_limit_bytes=VMEM_LIMIT)


def set_keys(keys):
    row = lax.broadcasted_iota(jnp.int32, (2 * HID, 2 * HID), 0)
    lane = lax.broadcasted_iota(jnp.int32, (2 * HID, 2 * HID), 1)
    keys[0] = row % 32 - lane // HID
    keys[1] = lane % 32 - row // HID


def with_sums(size, body):
    pl.run_scoped(body, *[pltpu.ACC(m)((size * 64, 2 * HID), jnp.float32) for m in (0, 0, 1, 1)])


def closure_scratch(planes, size):
    return [
        pltpu.VMEM((planes // size, size * 128, 2 * HID), jnp.bfloat16),
        pltpu.VMEM((2, 2 * HID, 2 * HID), jnp.int32),
    ]


def slab_shapes(count, n):
    return [jax.ShapeDtypeStruct((count, 3, n, 128), jnp.bfloat16)] * 4


def slab_call(state, velocity):
    n = state.shape[1]
    return pl.pallas_call(
        slab_kernel,
        out_shape=slab_shapes(NV + 1, n),
        in_specs=[VM] * 2,
        out_specs=[VM] * 4,
        compiler_params=PARAMS,
        name="slabs",
    )(state, velocity)


def depth_call(opening, state, extra, band, weights):
    n = state.shape[1]
    plane = lambda dtype: jax.ShapeDtypeStruct((n, 128, 128), dtype)
    shapes = [plane(jnp.float32), plane(jnp.bfloat16)]
    if opening:
        shapes += [plane(jnp.bfloat16), plane(jnp.float32)]
    args = (state, *extra, band, *weights)
    return pl.pallas_call(
        functools.partial(depth_kernel, opening),
        out_shape=shapes,
        in_specs=[VM] * len(args),
        out_specs=[VM] * len(shapes),
        scratch_shapes=[pltpu.VMEM((n, 128, 128), jnp.float32), pltpu.VMEM((EARLY, 128, 128), jnp.float32)] + closure_scratch(EARLY, DEPTH_SIZE),
        compiler_params=PARAMS,
        cost_estimate=pl.CostEstimate(flops=1 << 34, bytes_accessed=8 << 20, transcendentals=0),
        name="depth",
    )(*args)


def cross_call(state, velocity, parts, band, weights, halos, old):
    n = state.shape[1]
    last = old is not None
    args = (state, velocity, *parts, band, *weights, *halos) + ((old,) if last else ())
    shapes = [jax.ShapeDtypeStruct(state.shape, jnp.float32)]
    if not last:
        shapes += slab_shapes(NV, n)
    return pl.pallas_call(
        functools.partial(cross_kernel, last),
        out_shape=shapes,
        in_specs=[VM] * 2 + [ANY] + [VM] * (len(args) - 4) + [ANY if last else VM],
        out_specs=[ANY] + [VM] * (len(shapes) - 1),
        scratch_shapes=[pltpu.VMEM(state.shape, jnp.float32)] * 2
        + [pltpu.VMEM((n, 128, 128), jnp.float32)]
        + closure_scratch(n - EARLY, CROSS_SIZE)
        + [pltpu.VMEM((n, 128, 128), jnp.float32), pltpu.VMEM(state.shape, jnp.float32)]
        + [pltpu.SemaphoreType.DMA((2 + 4 * NV,))]
        + ([pltpu.VMEM(state.shape, jnp.float32)] if last else []),
        compiler_params=PARAMS,
        cost_estimate=pl.CostEstimate(flops=1 << 35, bytes_accessed=12 << 20, transcendentals=0),
        name="cross",
    )(*args)


def send(value, axis, up):
    n = lax.axis_size(axis)
    if up:
        return lax.ppermute(value, axis, [(i, (i + 1) % n) for i in range(n)])
    return lax.ppermute(value, axis, [((i + 1) % n, i) for i in range(n)])


def exchange(to_lo_x, to_hi_x, to_lo_y, to_hi_y):
    return [
        send(to_hi_x, "gx", True),
        send(to_lo_x, "gx", False),
        send(to_hi_y, "gy", True),
        send(to_lo_y, "gy", False),
    ]


def prepare(w_in, w_mid, w_deep, w_out, ny):
    half = jnp.asarray(0.5, jnp.bfloat16)
    two = jnp.eye(2, dtype=jnp.bfloat16)
    padded = jnp.pad((w_in.T * half).astype(jnp.float32), ((0, 1), (0, 0)))
    wsel = jnp.tile(jnp.repeat(padded, ny, axis=0), (1, 2))
    wmid = jnp.kron(two, w_mid.T * half)
    wdeep = jnp.kron(two, w_deep.T * half)
    wout = jnp.tile(jnp.repeat(w_out.T.astype(jnp.float32), ny, axis=1), (2, 1))
    return wsel, wmid, wdeep, wout


def shards(state, velocity, routes, w_in, w_mid, w_deep, w_out):
    ny = state.shape[2]
    cut = slab_call(state, velocity)
    halos = exchange(*cut)
    opening = halos
    weights = prepare(w_in, w_mid, w_deep, w_out, ny)
    member = (routes >= 0).astype(jnp.float32)
    band = jnp.repeat(member.transpose(0, 2, 1), BS, axis=1)
    band = jnp.tile(jnp.repeat(band, BS, axis=2), (1, 1, NV))

    rt, stb, vtb, ut = depth_call(True, state, (velocity,), band, weights)
    first, *cut = cross_call(state, velocity, (rt, stb, vtb), band, weights, halos, None)
    halos = exchange(*cut)
    rt, stb = depth_call(False, first, (vtb, ut), band, weights)
    return cross_call(first, velocity, (rt, stb, vtb), band, weights, halos + opening, state)[0]


def solution(mesh):
    placed = (
        P(None, "gx", "gy", None),
        P(None, "gx", "gy", None),
        P("gx", "gy", None),
        P(),
        P(),
        P(),
        P(),
    )
    return jax.shard_map(
        shards, mesh=mesh, in_specs=placed, out_specs=P(None, "gx", "gy", None), check_vma=False
    )
```

```python
import functools

import jax
import jax.numpy as jnp
from jax import lax
from jax.experimental import pallas as pl
from jax.experimental.pallas import tpu as pltpu
from jax.sharding import PartitionSpec as P

BS = 16
EPS = 1e-06
STEP = 0.25
NV = 4
NF = 7
HID = 128
PAIRS = 16
DEPTH_SIZE = 2
REGIONS = 4
LAG = 2
CROSS_SIZE = 2
EARLY = 8
WENO_TYPE = jnp.bfloat16
SILU_TYPE = jnp.bfloat16
TILE = 16
VMEM_LIMIT = 60 * 1024 * 1024


def reciprocal(x):
    return pl.reciprocal(x, approx=True)


def curvature(d1, d2, d3, d4):
    one = lambda x: jnp.asarray(x, d1.dtype)
    g2 = one(0.609375) * (d2 * d2) + one(0.75 * EPS)
    g3 = one(0.609375) * (d3 * d3) + one(0.75 * EPS)
    e0 = d1 - one(1.375) * d2
    e1 = d3 - one(0.625) * d2
    e2 = d4 - one(1.375) * d3
    r0 = reciprocal(e0 * e0 + g2)
    r1 = reciprocal(e1 * e1 + g2)
    r2 = reciprocal(e2 * e2 + g3)
    t0 = e0 + e1
    t2 = e2 + (d2 - one(0.625) * d3)
    w0 = r0 * r0
    w2 = one(1.5) * (r2 * r2)
    total = one(0.5) * w0 + one(3.0) * (r1 * r1) + w2
    return (w0 * t0 + w2 * t2) * reciprocal(total)


def face_flux(fd, vd, second, alpha, centre):
    rough = alpha.astype(WENO_TYPE)
    m = [rough * d for d in vd]
    p = [fd[j] + m[j] for j in range(4)]
    q = [fd[j] - m[j] for j in range(1, 5)]
    bend = (curvature(*p) - curvature(*q[::-1])).astype(jnp.float32)
    before, after, v_before, v_after = second
    rest = (before - after) + alpha * (v_after - v_before) - bend
    return centre + rest * (1.0 / 6.0)


class Sweep:
    def __init__(self, n, load_v, load_u, emit):
        self.last, self.load_v, self.load_u, self.emit = n + 3, load_v, load_u, emit

    def points(self):
        return range(-3, self.last)

    def advance(self, state, j, token):
        us, fs, vs, fds, vds, frough, vrough, vseconds, before = state
        u, v = self.load_u(j), self.load_v(j)
        if token is not None:
            u = u + token
        f = u * v
        if vs:
            fds = fds + [f - fs[-1]]
            vds = vds + [v - vs[-1]]
            frough = frough + [fds[-1].astype(WENO_TYPE)]
            vrough = vrough + [vds[-1].astype(WENO_TYPE)]
        if len(vds) > 1:
            vseconds = vseconds + [vds[-1] - vds[-2]]
        us, fs = us + [u], fs + [f]
        if len(frough) == 5:
            alpha = jnp.maximum(jnp.abs(us[0]), jnp.abs(us[1]))
            second = (fds[-4], fds[-2], vseconds[-3], vseconds[-2])
            flux = face_flux(frough, vrough, second, alpha, fs[0] + fs[1])
            if before:
                self.emit(j - 3, flux - before[0])
            before = [flux]
        return us[-3:], fs[-3:], [v], fds[-4:], vds[-1:], frough[-4:], vrough[-4:], vseconds[-3:], before


def silu_half(h):
    h = h.astype(SILU_TYPE)
    return (h + h * jnp.tanh(h)).astype(jnp.bfloat16)


def closure_part(pair, planes, size, st_ref, vt_ref, weights, tot_ref, hidden, keys, square, accs):
    wsel_ref, _, _, wout_ref = weights
    chunks = (planes[1] - planes[0]) // size
    half = size * 64
    zero = jnp.zeros((2 * HID, 2 * HID), jnp.float32)
    layers = (
        lambda: jnp.where(keys[0] == 2 * pair, wsel_ref[...], zero).astype(jnp.bfloat16),
        lambda: square[0],
        lambda: square[1],
        lambda: jnp.concatenate(
            [jnp.where(keys[1][:, :128] == 2 * pair, wout_ref[...], zero[:, :128]), zero[:, 128:]], axis=1
        ).astype(jnp.bfloat16),
    )
    waiting, token = [], None

    def push(layer):
        for m in range(2):
            pltpu.matmul_push_rhs(layers[layer](), layer % 2, m)

    def take(layer, c, r):
        for m in range(2):
            sums = pltpu.matmul_pop(accs[REGIONS * m + r])
            if layer < 3:
                hidden[c, pl.ds(m * half, half), :] = silu_half(sums)
            else:
                span = pl.ds(planes[0] + c * size + m * size // 2, size // 2)
                tot_ref[span] = tot_ref[span] + sums[:, :128].reshape(size // 2, 128, 128)
        return jnp.where(sums[-TILE:, :128] > 0.0, 0.0, -0.0)

    push(0)
    for layer in range(4):
        for c in range(chunks):
            r = (layer * chunks + c) % REGIONS
            for m in range(2):
                if layer == 0:
                    span = pl.ds(planes[0] + c * size + m * size // 2, size // 2)
                    lhs = jnp.concatenate([st_ref[span].reshape(half, 128), vt_ref[span].reshape(half, 128)], axis=1)
                else:
                    lhs = hidden[c, pl.ds(m * half, half), :]
                pltpu.matmul_acc_lhs(accs[REGIONS * m + r], lhs, layer % 2 if c == 0 else None)
            if c == 0 and layer < 3:
                push(layer + 1)
            waiting.append((layer, c, r))
            if len(waiting) > LAG or (layer < 3 and c == chunks - 1 and chunks <= LAG):
                token = take(*waiting.pop(0))
            yield token
    while waiting:
        yield take(*waiting.pop(0))


def together(closure, steps, sweeps):
    work = [(sweep, j) for sweep in sweeps for j in sweep.points()]
    costs = [1.0 if j > 1 else 0.15 for _, j in work]
    total, spent, at = sum(costs), 0.0, 0
    state, owner = None, None
    for i in range(steps):
        token = next(closure, None)
        while at < len(work) and (i == steps - 1 or spent + costs[at] / 2 < total * (i + 1) / steps):
            sweep, j = work[at]
            if sweep is not owner:
                state, owner = ([],) * 9, sweep
            state = sweep.advance(state, j, token)
            spent += costs[at]
            at += 1


def depth_kernel(opening, *refs):
    if opening:
        s_ref, v_ref, band_ref, *weights = refs[:7]
        rt_ref, stb_ref, vtb_ref, ut_ref, st, tot, hidden, keys, square = refs[7:]
    else:
        s_ref, vtb_ref, ut_ref, band_ref, *weights = refs[:8]
        rt_ref, stb_ref, st, tot, hidden, keys, square = refs[8:]
    nx, ny = s_ref.shape[1], s_ref.shape[2]

    @pl.loop(0, nx, unroll=4)
    def _(x):
        t = jnp.concatenate([s_ref[k, x] for k in range(NV)], axis=0).T
        st[x] = t
        stb_ref[x] = t.astype(jnp.bfloat16)
        if opening:
            w = v_ref[2, x]
            vt = jnp.concatenate([v_ref[0, x], v_ref[1, x], w, jnp.zeros_like(w)], axis=0).T
            vtb_ref[x] = vt.astype(jnp.bfloat16)
            ut_ref[x] = jnp.concatenate([0.5 * w] * NV, axis=0).T

    @pl.loop(0, EARLY, unroll=4)
    def _(x):
        tot[x] = jnp.zeros((128, 128), jnp.float32)

    st2 = st.reshape(nx * 128, 128)
    ut2 = ut_ref.reshape(nx * 128, 128)
    rt2 = rt_ref.reshape(nx * 128, 128)

    set_keys(keys)
    set_square(square, weights)

    def main(*accs):
        @pl.loop(0, PAIRS)
        def _(step):
            x0 = (step // 8) * TILE
            z0 = (step % 8) * 16

            def at(j):
                return pl.ds(x0 * 128 + ((z0 + j) & 127), TILE, stride=128)

            def emit(j, value):
                rt2[at(j), :] = -value

            column = Sweep(16, lambda j: st2[at(j), :], lambda j: ut2[at(j), :], emit)
            closure = closure_part(step, (0, EARLY), DEPTH_SIZE, stb_ref, vtb_ref, weights, tot, hidden, keys, square, accs)
            together(closure, EARLY // DEPTH_SIZE * 4 + LAG, (column,))

    with_sums(DEPTH_SIZE, main)

    @pl.loop(0, EARLY, unroll=4)
    def _(x):
        rt_ref[x] = rt_ref[x] + jnp.where(band_ref[x // BS] > 0, tot[x], 0.0)


def cross_kernel(last, *refs):
    s_ref, v_ref, rt_hbm, stb_ref, vtb_ref, band_ref, *weights = refs[:10]
    xlo, xhi, ylo, yhi = refs[10:14]
    rest = refs[14:] if not last else refs[18:]
    uxlo, uxhi, uylo, uyhi = (r.at[NV] for r in (refs[10:14] if not last else refs[14:18]))
    if last:
        old_hbm, out_hbm, dx, dy, tot, hidden, keys, square, rt_ref, out_ref, sems, old_ref = rest
    else:
        out_hbm, *slabs = rest[:5]
        dx, dy, tot, hidden, keys, square, rt_ref, out_ref, sems = rest[5:]
    nx, ny = s_ref.shape[1], s_ref.shape[2]
    s2 = s_ref.reshape(NV * nx * ny, 128)
    v2 = v_ref.reshape(3 * nx * ny, 128)
    dy2 = dy.reshape(NV * nx * ny, 128)
    coming = [pltpu.make_async_copy(rt_hbm, rt_ref, sems.at[0])]
    if last:
        coming.append(pltpu.make_async_copy(old_hbm, old_ref, sems.at[1]))
    for copy in coming:
        copy.start()

    @pl.loop(EARLY, nx, unroll=4)
    def _(x):
        tot[x] = jnp.zeros((128, 128), jnp.float32)

    set_keys(keys)
    set_square(square, weights)

    def main(*accs):
        @pl.loop(0, PAIRS)
        def _(step):
            k = step // 4
            c0 = pl.multiple_of((step // 2 % 2) * TILE, TILE)
            cs = pl.ds(c0, TILE)
            base = (step % 2) * 16

            def wide(ref, *index):
                return ref[(*index, cs, slice(None))].astype(jnp.float32)

            def point(j, n, inner, lo, hi):
                if j < 0:
                    return jnp.where(base == 0, lo(j + 3), inner(jnp.maximum(base + j, 0)))
                if j >= 16:
                    return jnp.where(base == 0, inner(jnp.minimum(base + j, n - 1)), hi(j - 16))
                return inner(base + j)

            def column(lead, y):
                return pl.ds((lead * nx + c0) * ny + y, TILE, stride=ny)

            def yv(j):
                return point(j, ny, lambda y: s2[column(k, y), :], lambda i: wide(ylo, k, i), lambda i: wide(yhi, k, i))

            def yu(j):
                return 0.5 * point(j, ny, lambda y: v2[column(1, y), :], lambda i: wide(uylo, i), lambda i: wide(uyhi, i))

            def yemit(j, value):
                dy2[column(k, base + j), :] = value

            def xv(j):
                return point(j, nx, lambda x: s_ref[k, x, cs, :], lambda i: wide(xlo, k, i), lambda i: wide(xhi, k, i))

            def xu(j):
                return 0.5 * point(j, nx, lambda x: v_ref[0, x, cs, :], lambda i: wide(uxlo, i), lambda i: wide(uxhi, i))

            def xemit(j, value):
                dx[k, base + j, cs, :] = value

            closure = closure_part(step, (EARLY, nx), CROSS_SIZE, stb_ref, vtb_ref, weights, tot, hidden, keys, square, accs)
            together(
                closure,
                (nx - EARLY) // CROSS_SIZE * 4 + LAG,
                (Sweep(16, yv, yu, yemit), Sweep(16, xv, xu, xemit)),
            )

    with_sums(CROSS_SIZE, main)

    def finish(x, rate_t):
        back = rate_t.T
        for k in range(NV):
            rate = back[k * ny : (k + 1) * ny] - (dx[k, x] + dy[k, x])
            stepped = s_ref[k, x] + STEP * rate
            if last:
                stepped = 0.75 * old_ref[k, x] + 0.25 * stepped
            out_ref[k, x] = stepped

    for copy in coming:
        copy.wait()
    going = []
    for part in range(4):
        lo, hi = part * nx // 4, (part + 1) * nx // 4

        @pl.loop(lo, hi, unroll=4)
        def _(x):
            rate_t = rt_ref[x]
            if lo >= EARLY:
                rate_t = rate_t + jnp.where(band_ref[x // BS] > 0, tot[x], 0.0)
            finish(x, rate_t)

        for k in range(NV):
            span = pl.ds(lo, hi - lo)
            going.append(pltpu.make_async_copy(out_ref.at[k, span], out_hbm.at[k, span], sems.at[2 + part * NV + k]))
            going[-1].start()

    if not last:
        cut_slabs(out_ref, [(k, k) for k in range(NV)], *slabs)
    for copy in going:
        copy.wait()


def cut_slabs(ref, which, to_lo_x, to_hi_x, to_lo_y, to_hi_y):
    lead, nx, ny = ref.shape[:3]
    flat = ref.reshape(lead * nx * ny, 128)
    for src, dst in which:
        for j in range(3):
            to_lo_x[dst, j] = ref[src, j].astype(jnp.bfloat16)
            to_hi_x[dst, j] = ref[src, nx - 3 + j].astype(jnp.bfloat16)
            for target, y in ((to_lo_y, j), (to_hi_y, ny - 3 + j)):
                target[dst, j] = flat[pl.ds(src * nx * ny + y, nx, stride=ny), :].astype(jnp.bfloat16)


def slab_kernel(s_ref, v_ref, *slabs):
    cut_slabs(s_ref, [(k, k) for k in range(NV)], *slabs)
    nx, ny = v_ref.shape[1], v_ref.shape[2]
    flat = v_ref.reshape(3 * nx * ny, 128)
    for j in range(3):
        slabs[0][NV, j] = v_ref[0, j].astype(jnp.bfloat16)
        slabs[1][NV, j] = v_ref[0, nx - 3 + j].astype(jnp.bfloat16)
        slabs[2][NV, j] = flat[pl.ds(nx * ny + j, nx, stride=ny), :].astype(jnp.bfloat16)
        slabs[3][NV, j] = flat[pl.ds(nx * ny + ny - 3 + j, nx, stride=ny), :].astype(jnp.bfloat16)


VM = pl.BlockSpec(memory_space=pltpu.VMEM)
ANY = pl.BlockSpec(memory_space=pl.ANY)
PARAMS = pltpu.CompilerParams(vmem_limit_bytes=VMEM_LIMIT)


def set_keys(keys):
    row = lax.broadcasted_iota(jnp.int32, (2 * HID, 2 * HID), 0)
    lane = lax.broadcasted_iota(jnp.int32, (2 * HID, 2 * HID), 1)
    keys[0] = row % 32 - lane // HID
    keys[1] = lane % 32 - row // HID


def set_square(square, weights):
    for i in range(2):
        part = (0.5 * weights[1 + i][...].astype(jnp.float32)).T.astype(jnp.bfloat16)
        none = jnp.zeros_like(part)
        square[i] = jnp.concatenate(
            [jnp.concatenate([part, none], axis=1), jnp.concatenate([none, part], axis=1)], axis=0
        )


def with_sums(size, body):
    pl.run_scoped(body, *[pltpu.ACC(m)((size * 64, 2 * HID), jnp.float32) for m in range(2) for _ in range(REGIONS)])


def closure_scratch(planes, size):
    return [
        pltpu.VMEM((planes // size, size * 128, 2 * HID), jnp.bfloat16),
        pltpu.VMEM((2, 2 * HID, 2 * HID), jnp.int32),
        pltpu.VMEM((2, 2 * HID, 2 * HID), jnp.bfloat16),
    ]


def slab_shapes(count, n):
    return [jax.ShapeDtypeStruct((count, 3, n, 128), jnp.bfloat16)] * 4


def slab_call(state, velocity):
    n = state.shape[1]
    return pl.pallas_call(
        slab_kernel,
        out_shape=slab_shapes(NV + 1, n),
        in_specs=[VM] * 2,
        out_specs=[VM] * 4,
        compiler_params=PARAMS,
        name="slabs",
    )(state, velocity)


def depth_call(opening, state, extra, band, weights):
    n = state.shape[1]
    plane = lambda dtype: jax.ShapeDtypeStruct((n, 128, 128), dtype)
    shapes = [plane(jnp.float32), plane(jnp.bfloat16)]
    if opening:
        shapes += [plane(jnp.bfloat16), plane(jnp.float32)]
    args = (state, *extra, band, *weights)
    return pl.pallas_call(
        functools.partial(depth_kernel, opening),
        out_shape=shapes,
        in_specs=[VM] * len(args),
        out_specs=[VM] * len(shapes),
        scratch_shapes=[pltpu.VMEM((n, 128, 128), jnp.float32), pltpu.VMEM((EARLY, 128, 128), jnp.float32)] + closure_scratch(EARLY, DEPTH_SIZE),
        compiler_params=PARAMS,
        cost_estimate=pl.CostEstimate(flops=1 << 34, bytes_accessed=8 << 20, transcendentals=0),
        name="depth",
    )(*args)


def cross_call(state, velocity, parts, band, weights, halos, old):
    n = state.shape[1]
    last = old is not None
    args = (state, velocity, *parts, band, *weights, *halos) + ((old,) if last else ())
    shapes = [jax.ShapeDtypeStruct(state.shape, jnp.float32)]
    if not last:
        shapes += slab_shapes(NV, n)
    return pl.pallas_call(
        functools.partial(cross_kernel, last),
        out_shape=shapes,
        in_specs=[VM] * 2 + [ANY] + [VM] * (len(args) - 4) + [ANY if last else VM],
        out_specs=[ANY] + [VM] * (len(shapes) - 1),
        scratch_shapes=[pltpu.VMEM(state.shape, jnp.float32)] * 2
        + [pltpu.VMEM((n, 128, 128), jnp.float32)]
        + closure_scratch(n - EARLY, CROSS_SIZE)
        + [pltpu.VMEM((n, 128, 128), jnp.float32), pltpu.VMEM(state.shape, jnp.float32)]
        + [pltpu.SemaphoreType.DMA((2 + 4 * NV,))]
        + ([pltpu.VMEM(state.shape, jnp.float32)] if last else []),
        compiler_params=PARAMS,
        cost_estimate=pl.CostEstimate(flops=1 << 35, bytes_accessed=12 << 20, transcendentals=0),
        name="cross",
    )(*args)


def send(value, axis, up):
    n = lax.axis_size(axis)
    if up:
        return lax.ppermute(value, axis, [(i, (i + 1) % n) for i in range(n)])
    return lax.ppermute(value, axis, [((i + 1) % n, i) for i in range(n)])


def exchange(to_lo_x, to_hi_x, to_lo_y, to_hi_y):
    return [
        send(to_hi_x, "gx", True),
        send(to_lo_x, "gx", False),
        send(to_hi_y, "gy", True),
        send(to_lo_y, "gy", False),
    ]


def prepare(w_in, w_mid, w_deep, w_out, ny):
    half = jnp.asarray(0.5, jnp.bfloat16)
    padded = jnp.pad((w_in.T * half).astype(jnp.float32), ((0, 1), (0, 0)))
    wsel = jnp.tile(jnp.repeat(padded, ny, axis=0), (1, 2))
    wout = jnp.tile(jnp.repeat(w_out.T.astype(jnp.float32), ny, axis=1), (2, 1))
    return wsel, w_mid, w_deep, wout


def shards(state, velocity, routes, w_in, w_mid, w_deep, w_out):
    ny = state.shape[2]
    cut = slab_call(state, velocity)
    halos = exchange(*cut)
    opening = halos
    weights = prepare(w_in, w_mid, w_deep, w_out, ny)
    member = (routes >= 0).astype(jnp.float32)
    band = jnp.repeat(member.transpose(0, 2, 1), BS, axis=1)
    band = jnp.tile(jnp.repeat(band, BS, axis=2), (1, 1, NV))

    rt, stb, vtb, ut = depth_call(True, state, (velocity,), band, weights)
    first, *cut = cross_call(state, velocity, (rt, stb, vtb), band, weights, halos, None)
    halos = exchange(*cut)
    rt, stb = depth_call(False, first, (vtb, ut), band, weights)
    return cross_call(first, velocity, (rt, stb, vtb), band, weights, halos + opening, state)[0]


def solution(mesh):
    placed = (
        P(None, "gx", "gy", None),
        P(None, "gx", "gy", None),
        P("gx", "gy", None),
        P(),
        P(),
        P(),
        P(),
    )
    return jax.shard_map(
        shards, mesh=mesh, in_specs=placed, out_specs=P(None, "gx", "gy", None), check_vma=False
    )
```

```python
import functools

import jax
import jax.numpy as jnp
from jax import lax
from jax.experimental import pallas as pl
from jax.experimental.pallas import tpu as pltpu
from jax.sharding import PartitionSpec as P

BS = 16
EPS = 1e-06
STEP = 0.25
NV = 4
NF = 7
HID = 128
PAIRS = 16
DEPTH_SIZE = 2
REGIONS = 4
DEPTH_AHEAD = 3
CROSS_AHEAD = 0
LAG = 2
CROSS_SIZE = 2
EARLY = 8
WENO_TYPE = jnp.bfloat16
SILU_TYPE = jnp.bfloat16
TILE = 16
VMEM_LIMIT = 60 * 1024 * 1024


def reciprocal(x):
    return pl.reciprocal(x, approx=True)


def curvature(d1, d2, d3, d4):
    one = lambda x: jnp.asarray(x, d1.dtype)
    g2 = one(0.609375) * (d2 * d2) + one(0.75 * EPS)
    g3 = one(0.609375) * (d3 * d3) + one(0.75 * EPS)
    e0 = d1 - one(1.375) * d2
    e1 = d3 - one(0.625) * d2
    e2 = d4 - one(1.375) * d3
    r0 = reciprocal(e0 * e0 + g2)
    r1 = reciprocal(e1 * e1 + g2)
    r2 = reciprocal(e2 * e2 + g3)
    t0 = e0 + e1
    t2 = e2 + (d2 - one(0.625) * d3)
    w0 = r0 * r0
    w2 = one(1.5) * (r2 * r2)
    total = one(0.5) * w0 + one(3.0) * (r1 * r1) + w2
    return (w0 * t0 + w2 * t2) * reciprocal(total)


def face_flux(fd, vd, second, alpha, centre):
    rough = alpha.astype(WENO_TYPE)
    m = [rough * d for d in vd]
    p = [fd[j] + m[j] for j in range(4)]
    q = [fd[j] - m[j] for j in range(1, 5)]
    bend = (curvature(*p) - curvature(*q[::-1])).astype(jnp.float32)
    before, after, v_before, v_after = second
    rest = (before - after) + alpha * (v_after - v_before) - bend
    return centre + rest * (1.0 / 6.0)


class Sweep:
    def __init__(self, n, load_v, load_u, emit):
        self.last, self.load_v, self.load_u, self.emit = n + 3, load_v, load_u, emit

    def points(self):
        return range(-3, self.last)

    def advance(self, state, j, token):
        us, fs, vs, fds, vds, frough, vrough, vseconds, before = state
        u, v = self.load_u(j), self.load_v(j)
        if token is not None:
            u = u + token
        f = u * v
        if vs:
            fds = fds + [f - fs[-1]]
            vds = vds + [v - vs[-1]]
            frough = frough + [fds[-1].astype(WENO_TYPE)]
            vrough = vrough + [vds[-1].astype(WENO_TYPE)]
        if len(vds) > 1:
            vseconds = vseconds + [vds[-1] - vds[-2]]
        us, fs = us + [u], fs + [f]
        if len(frough) == 5:
            alpha = jnp.maximum(jnp.abs(us[0]), jnp.abs(us[1]))
            second = (fds[-4], fds[-2], vseconds[-3], vseconds[-2])
            flux = face_flux(frough, vrough, second, alpha, fs[0] + fs[1])
            if before:
                self.emit(j - 3, flux - before[0])
            before = [flux]
        return us[-3:], fs[-3:], [v], fds[-4:], vds[-1:], frough[-4:], vrough[-4:], vseconds[-3:], before


def silu_half(h):
    h = h.astype(SILU_TYPE)
    return (h + h * jnp.tanh(h)).astype(jnp.bfloat16)


def closure_part(pair, planes, size, st_ref, vt_ref, weights, tot_ref, hidden, keys, square, accs):
    wsel_ref, _, _, wout_ref = weights
    chunks = (planes[1] - planes[0]) // size
    half = size * 64
    zero = jnp.zeros((2 * HID, 2 * HID), jnp.float32)
    layers = (
        lambda: jnp.where(keys[0] == 2 * pair, wsel_ref[...], zero).astype(jnp.bfloat16),
        lambda: square[0],
        lambda: square[1],
        lambda: jnp.concatenate(
            [jnp.where(keys[1][:, :128] == 2 * pair, wout_ref[...], zero[:, :128]), zero[:, 128:]], axis=1
        ).astype(jnp.bfloat16),
    )
    waiting, token = [], None

    def push(layer):
        for m in range(2):
            pltpu.matmul_push_rhs(layers[layer](), layer % 2, m)

    def take(layer, c, r):
        for m in range(2):
            sums = pltpu.matmul_pop(accs[REGIONS * m + r])
            if layer < 3:
                hidden[c, pl.ds(m * half, half), :] = silu_half(sums)
            else:
                span = pl.ds(planes[0] + c * size + m * size // 2, size // 2)
                tot_ref[span] = tot_ref[span] + sums[:, :128].reshape(size // 2, 128, 128)
        return jnp.where(sums[-TILE:, :128] > 0.0, 0.0, -0.0)

    push(0)
    for layer in range(4):
        for c in range(chunks):
            r = (layer * chunks + c) % REGIONS
            for m in range(2):
                if layer == 0:
                    span = pl.ds(planes[0] + c * size + m * size // 2, size // 2)
                    lhs = jnp.concatenate([st_ref[span].reshape(half, 128), vt_ref[span].reshape(half, 128)], axis=1)
                else:
                    lhs = hidden[c, pl.ds(m * half, half), :]
                pltpu.matmul_acc_lhs(accs[REGIONS * m + r], lhs, layer % 2 if c == 0 else None)
            if c == 0 and layer < 3:
                push(layer + 1)
            waiting.append((layer, c, r))
            if len(waiting) > LAG or (layer < 3 and c == chunks - 1 and chunks <= LAG):
                token = take(*waiting.pop(0))
            yield token
    while waiting:
        yield take(*waiting.pop(0))


def together(closure, steps, ahead, sweeps):
    work = [(sweep, j) for sweep in sweeps for j in sweep.points()]
    costs = [1.0 if j > 1 else 0.15 for _, j in work]
    total, spent, at = sum(costs), 0.0, 0
    state, owner = None, None
    for i in range(steps):
        token = next(closure, None)
        while at < len(work) and (i == steps - 1 or spent + costs[at] / 2 < total * (i + 1 + ahead) / (steps + ahead)):
            sweep, j = work[at]
            if sweep is not owner:
                state, owner = ([],) * 9, sweep
            state = sweep.advance(state, j, token)
            spent += costs[at]
            at += 1


def depth_kernel(opening, *refs):
    if opening:
        s_ref, v_ref, band_ref, *weights = refs[:7]
        rt_ref, stb_hbm, vtb_hbm, ut_hbm, st, tot, hidden, keys, square, stb_ref, vtb_ref, ut_ref, sems = refs[7:]
        coming = []
        going = [(vtb_ref, vtb_hbm, sems.at[0]), (ut_ref, ut_hbm, sems.at[1])]
    else:
        s_ref, vtb_hbm, ut_hbm, band_ref, *weights = refs[:8]
        rt_ref, stb_hbm, st, tot, hidden, keys, square, stb_ref, vtb_ref, ut_ref, sems = refs[8:]
        coming = [(vtb_hbm, vtb_ref, sems.at[0]), (ut_hbm, ut_ref, sems.at[1])]
        going = []
    coming = [pltpu.make_async_copy(*each) for each in coming]
    going = [pltpu.make_async_copy(*each) for each in going + [(stb_ref, stb_hbm, sems.at[2])]]
    for copy in coming:
        copy.start()
    nx, ny = s_ref.shape[1], s_ref.shape[2]

    @pl.loop(0, nx, unroll=4)
    def _(x):
        t = jnp.concatenate([s_ref[k, x] for k in range(NV)], axis=0).T
        st[x] = t
        stb_ref[x] = t.astype(jnp.bfloat16)
        if opening:
            w = v_ref[2, x]
            vt = jnp.concatenate([v_ref[0, x], v_ref[1, x], w, jnp.zeros_like(w)], axis=0).T
            vtb_ref[x] = vt.astype(jnp.bfloat16)
            ut_ref[x] = jnp.concatenate([0.5 * w] * NV, axis=0).T

    for copy in going:
        copy.start()

    @pl.loop(0, EARLY, unroll=4)
    def _(x):
        tot[x] = jnp.zeros((128, 128), jnp.float32)

    st2 = st.reshape(nx * 128, 128)
    ut2 = ut_ref.reshape(nx * 128, 128)
    rt2 = rt_ref.reshape(nx * 128, 128)

    set_keys(keys)
    set_square(square, weights)
    for copy in coming:
        copy.wait()

    def main(*accs):
        @pl.loop(0, PAIRS)
        def _(step):
            x0 = (step // 8) * TILE
            z0 = (step % 8) * 16

            def at(j):
                return pl.ds(x0 * 128 + ((z0 + j) & 127), TILE, stride=128)

            def emit(j, value):
                rt2[at(j), :] = -value

            column = Sweep(16, lambda j: st2[at(j), :], lambda j: ut2[at(j), :], emit)
            closure = closure_part(step, (0, EARLY), DEPTH_SIZE, stb_ref, vtb_ref, weights, tot, hidden, keys, square, accs)
            together(closure, EARLY // DEPTH_SIZE * 4 + LAG, DEPTH_AHEAD, (column,))

    with_sums(DEPTH_SIZE, main)

    @pl.loop(0, EARLY, unroll=4)
    def _(x):
        rt_ref[x] = rt_ref[x] + jnp.where(band_ref[x // BS] > 0, tot[x], 0.0)

    for copy in going:
        copy.wait()


def cross_kernel(last, *refs):
    s_ref, v_ref, rt_hbm, stb_ref, vtb_ref, band_ref, *weights = refs[:10]
    xlo, xhi, ylo, yhi = refs[10:14]
    rest = refs[14:] if not last else refs[18:]
    uxlo, uxhi, uylo, uyhi = (r.at[NV] for r in (refs[10:14] if not last else refs[14:18]))
    if last:
        old_hbm, out_hbm, dx, dy, tot, hidden, keys, square, rt_ref, out_ref, sems, old_ref = rest
    else:
        out_hbm, *slabs = rest[:5]
        dx, dy, tot, hidden, keys, square, rt_ref, out_ref, sems = rest[5:]
    nx, ny = s_ref.shape[1], s_ref.shape[2]
    s2 = s_ref.reshape(NV * nx * ny, 128)
    v2 = v_ref.reshape(3 * nx * ny, 128)
    dy2 = dy.reshape(NV * nx * ny, 128)
    coming = [pltpu.make_async_copy(rt_hbm, rt_ref, sems.at[0])]
    if last:
        coming.append(pltpu.make_async_copy(old_hbm, old_ref, sems.at[1]))
    for copy in coming:
        copy.start()

    @pl.loop(EARLY, nx, unroll=4)
    def _(x):
        tot[x] = jnp.zeros((128, 128), jnp.float32)

    set_keys(keys)
    set_square(square, weights)

    def main(*accs):
        @pl.loop(0, PAIRS)
        def _(step):
            k = step // 4
            c0 = pl.multiple_of((step // 2 % 2) * TILE, TILE)
            cs = pl.ds(c0, TILE)
            base = (step % 2) * 16

            def wide(ref, *index):
                return ref[(*index, cs, slice(None))].astype(jnp.float32)

            def point(j, n, inner, lo, hi):
                if j < 0:
                    return jnp.where(base == 0, lo(j + 3), inner(jnp.maximum(base + j, 0)))
                if j >= 16:
                    return jnp.where(base == 0, inner(jnp.minimum(base + j, n - 1)), hi(j - 16))
                return inner(base + j)

            def column(lead, y):
                return pl.ds((lead * nx + c0) * ny + y, TILE, stride=ny)

            def yv(j):
                return point(j, ny, lambda y: s2[column(k, y), :], lambda i: wide(ylo, k, i), lambda i: wide(yhi, k, i))

            def yu(j):
                return 0.5 * point(j, ny, lambda y: v2[column(1, y), :], lambda i: wide(uylo, i), lambda i: wide(uyhi, i))

            def yemit(j, value):
                dy2[column(k, base + j), :] = value

            def xv(j):
                return point(j, nx, lambda x: s_ref[k, x, cs, :], lambda i: wide(xlo, k, i), lambda i: wide(xhi, k, i))

            def xu(j):
                return 0.5 * point(j, nx, lambda x: v_ref[0, x, cs, :], lambda i: wide(uxlo, i), lambda i: wide(uxhi, i))

            def xemit(j, value):
                dx[k, base + j, cs, :] = value

            closure = closure_part(step, (EARLY, nx), CROSS_SIZE, stb_ref, vtb_ref, weights, tot, hidden, keys, square, accs)
            together(
                closure,
                (nx - EARLY) // CROSS_SIZE * 4 + LAG,
                CROSS_AHEAD,
                (Sweep(16, yv, yu, yemit), Sweep(16, xv, xu, xemit)),
            )

    with_sums(CROSS_SIZE, main)

    def finish(x, rate_t):
        back = rate_t.T
        for k in range(NV):
            rate = back[k * ny : (k + 1) * ny] - (dx[k, x] + dy[k, x])
            stepped = s_ref[k, x] + STEP * rate
            if last:
                stepped = 0.75 * old_ref[k, x] + 0.25 * stepped
            out_ref[k, x] = stepped

    for copy in coming:
        copy.wait()
    going = []
    for part in range(4):
        lo, hi = part * nx // 4, (part + 1) * nx // 4

        @pl.loop(lo, hi, unroll=4)
        def _(x):
            rate_t = rt_ref[x]
            if lo >= EARLY:
                rate_t = rate_t + jnp.where(band_ref[x // BS] > 0, tot[x], 0.0)
            finish(x, rate_t)

        for k in range(NV):
            span = pl.ds(lo, hi - lo)
            going.append(pltpu.make_async_copy(out_ref.at[k, span], out_hbm.at[k, span], sems.at[2 + part * NV + k]))
            going[-1].start()

    if not last:
        cut_slabs(out_ref, [(k, k) for k in range(NV)], *slabs)
    for copy in going:
        copy.wait()


def cut_slabs(ref, which, to_lo_x, to_hi_x, to_lo_y, to_hi_y):
    lead, nx, ny = ref.shape[:3]
    flat = ref.reshape(lead * nx * ny, 128)
    for src, dst in which:
        for j in range(3):
            to_lo_x[dst, j] = ref[src, j].astype(jnp.bfloat16)
            to_hi_x[dst, j] = ref[src, nx - 3 + j].astype(jnp.bfloat16)
            for target, y in ((to_lo_y, j), (to_hi_y, ny - 3 + j)):
                target[dst, j] = flat[pl.ds(src * nx * ny + y, nx, stride=ny), :].astype(jnp.bfloat16)


def slab_kernel(s_ref, v_ref, *slabs):
    cut_slabs(s_ref, [(k, k) for k in range(NV)], *slabs)
    nx, ny = v_ref.shape[1], v_ref.shape[2]
    flat = v_ref.reshape(3 * nx * ny, 128)
    for j in range(3):
        slabs[0][NV, j] = v_ref[0, j].astype(jnp.bfloat16)
        slabs[1][NV, j] = v_ref[0, nx - 3 + j].astype(jnp.bfloat16)
        slabs[2][NV, j] = flat[pl.ds(nx * ny + j, nx, stride=ny), :].astype(jnp.bfloat16)
        slabs[3][NV, j] = flat[pl.ds(nx * ny + ny - 3 + j, nx, stride=ny), :].astype(jnp.bfloat16)


VM = pl.BlockSpec(memory_space=pltpu.VMEM)
ANY = pl.BlockSpec(memory_space=pl.ANY)
PARAMS = pltpu.CompilerParams(vmem_limit_bytes=VMEM_LIMIT)


def set_keys(keys):
    row = lax.broadcasted_iota(jnp.int32, (2 * HID, 2 * HID), 0)
    lane = lax.broadcasted_iota(jnp.int32, (2 * HID, 2 * HID), 1)
    keys[0] = row % 32 - lane // HID
    keys[1] = lane % 32 - row // HID


def set_square(square, weights):
    for i in range(2):
        part = (0.5 * weights[1 + i][...].astype(jnp.float32)).T.astype(jnp.bfloat16)
        none = jnp.zeros_like(part)
        square[i] = jnp.concatenate(
            [jnp.concatenate([part, none], axis=1), jnp.concatenate([none, part], axis=1)], axis=0
        )


def with_sums(size, body):
    pl.run_scoped(body, *[pltpu.ACC(m)((size * 64, 2 * HID), jnp.float32) for m in range(2) for _ in range(REGIONS)])


def closure_scratch(planes, size):
    return [
        pltpu.VMEM((planes // size, size * 128, 2 * HID), jnp.bfloat16),
        pltpu.VMEM((2, 2 * HID, 2 * HID), jnp.int32),
        pltpu.VMEM((2, 2 * HID, 2 * HID), jnp.bfloat16),
    ]


def slab_shapes(count, n):
    return [jax.ShapeDtypeStruct((count, 3, n, 128), jnp.bfloat16)] * 4


def slab_call(state, velocity):
    n = state.shape[1]
    return pl.pallas_call(
        slab_kernel,
        out_shape=slab_shapes(NV + 1, n),
        in_specs=[VM] * 2,
        out_specs=[VM] * 4,
        compiler_params=PARAMS,
        name="slabs",
    )(state, velocity)


def depth_call(opening, state, extra, band, weights):
    n = state.shape[1]
    plane = lambda dtype: jax.ShapeDtypeStruct((n, 128, 128), dtype)
    shapes = [plane(jnp.float32), plane(jnp.bfloat16)]
    if opening:
        shapes += [plane(jnp.bfloat16), plane(jnp.float32)]
    args = (state, *extra, band, *weights)
    return pl.pallas_call(
        functools.partial(depth_kernel, opening),
        out_shape=shapes,
        in_specs=[VM, VM if opening else ANY] + [VM if opening else ANY] * (not opening) + [VM] * (len(args) - 2 - (not opening)),
        out_specs=[VM] + [ANY] * (len(shapes) - 1),
        scratch_shapes=[pltpu.VMEM((n, 128, 128), jnp.float32), pltpu.VMEM((EARLY, 128, 128), jnp.float32)] + closure_scratch(EARLY, DEPTH_SIZE)
        + [pltpu.VMEM((n, 128, 128), t) for t in (jnp.bfloat16, jnp.bfloat16, jnp.float32)]
        + [pltpu.SemaphoreType.DMA((3,))],
        compiler_params=PARAMS,
        cost_estimate=pl.CostEstimate(flops=1 << 34, bytes_accessed=8 << 20, transcendentals=0),
        name="depth",
    )(*args)


def cross_call(state, velocity, parts, band, weights, halos, old):
    n = state.shape[1]
    last = old is not None
    args = (state, velocity, *parts, band, *weights, *halos) + ((old,) if last else ())
    shapes = [jax.ShapeDtypeStruct(state.shape, jnp.float32)]
    if not last:
        shapes += slab_shapes(NV, n)
    return pl.pallas_call(
        functools.partial(cross_kernel, last),
        out_shape=shapes,
        in_specs=[VM] * 2 + [ANY] + [VM] * (len(args) - 4) + [ANY if last else VM],
        out_specs=[ANY] + [VM] * (len(shapes) - 1),
        scratch_shapes=[pltpu.VMEM(state.shape, jnp.float32)] * 2
        + [pltpu.VMEM((n, 128, 128), jnp.float32)]
        + closure_scratch(n - EARLY, CROSS_SIZE)
        + [pltpu.VMEM((n, 128, 128), jnp.float32), pltpu.VMEM(state.shape, jnp.float32)]
        + [pltpu.SemaphoreType.DMA((2 + 4 * NV,))]
        + ([pltpu.VMEM(state.shape, jnp.float32)] if last else []),
        compiler_params=PARAMS,
        cost_estimate=pl.CostEstimate(flops=1 << 35, bytes_accessed=12 << 20, transcendentals=0),
        name="cross",
    )(*args)


def send(value, axis, up):
    n = lax.axis_size(axis)
    if up:
        return lax.ppermute(value, axis, [(i, (i + 1) % n) for i in range(n)])
    return lax.ppermute(value, axis, [((i + 1) % n, i) for i in range(n)])


def exchange(to_lo_x, to_hi_x, to_lo_y, to_hi_y):
    return [
        send(to_hi_x, "gx", True),
        send(to_lo_x, "gx", False),
        send(to_hi_y, "gy", True),
        send(to_lo_y, "gy", False),
    ]


def prepare(w_in, w_mid, w_deep, w_out, ny):
    half = jnp.asarray(0.5, jnp.bfloat16)
    padded = jnp.pad((w_in.T * half).astype(jnp.float32), ((0, 1), (0, 0)))
    wsel = jnp.tile(jnp.repeat(padded, ny, axis=0), (1, 2))
    wout = jnp.tile(jnp.repeat(w_out.T.astype(jnp.float32), ny, axis=1), (2, 1))
    return wsel, w_mid, w_deep, wout


def shards(state, velocity, routes, w_in, w_mid, w_deep, w_out):
    ny = state.shape[2]
    cut = slab_call(state, velocity)
    halos = exchange(*cut)
    opening = halos
    weights = prepare(w_in, w_mid, w_deep, w_out, ny)
    member = (routes >= 0).astype(jnp.float32)
    band = jnp.repeat(member.transpose(0, 2, 1), BS, axis=1)
    band = jnp.tile(jnp.repeat(band, BS, axis=2), (1, 1, NV))

    rt, stb, vtb, ut = depth_call(True, state, (velocity,), band, weights)
    first, *cut = cross_call(state, velocity, (rt, stb, vtb), band, weights, halos, None)
    halos = exchange(*cut)
    rt, stb = depth_call(False, first, (vtb, ut), band, weights)
    return cross_call(first, velocity, (rt, stb, vtb), band, weights, halos + opening, state)[0]


def solution(mesh):
    placed = (
        P(None, "gx", "gy", None),
        P(None, "gx", "gy", None),
        P("gx", "gy", None),
        P(),
        P(),
        P(),
        P(),
    )
    return jax.shard_map(
        shards, mesh=mesh, in_specs=placed, out_specs=P(None, "gx", "gy", None), check_vma=False
    )
```
